32 devices in a mesh: expert: 8 (over z, x), tensor: 4 (over y, core).
Axes of the slice: x: 2, y: 2, z: 4, core: 2. Of those that a mesh axis runs over, the one named last changes fastest.
Arguments:
- tokens: bfloat16 [512, 3072], P('expert', 'tensor'), may hold values from -6 to 6
- grad_out: bfloat16 [512, 3072], P('expert', 'tensor'), may hold values from -3 to 3
- probs: bfloat16 [512, 4], P('expert'), may hold values from 0.049804688 to 0.5
- routes: int32 [512, 4], P('expert'), may hold values from 0 to 7, all different within a row; in each aligned block of 64 rows (0 to 63, 64 to 127, ...) at most 40 rows name the same one
- gate_weight: bfloat16 [8, 5376, 3072], P('expert', 'tensor'), may hold values from -0.109375 to 0.109375
- up_weight: bfloat16 [8, 5376, 3072], P('expert', 'tensor'), may hold values from -0.109375 to 0.109375
- down_weight: bfloat16 [8, 5376, 3072], P('expert', 'tensor'), may hold values from -0.078125 to 0.078125
Outputs:
- d_tokens: bfloat16 [512, 3072], P('expert', 'tensor')
- d_probs: float32 [512, 4], P('expert')
- d_down: bfloat16 [8, 5376, 3072], P('expert', 'tensor')
The draws below stay inside these ranges and needn't reach their ends.
Inputs may be any that keep to these rules, and one draw needn't show every extreme that they name: Each token's 4 experts differ. Among the 64 tokens of one index of expert, no expert is named by more than 40 routes, a bound that some block reaches of them.
All inputs are finite; a program needn't handle non-finite values.
Results may differ from the reference program's by a relative error of at most 0.007.
Values may be sent and summed in bfloat16 or wider, within the bound.
A program may use at most 128 MiB of HBM per device.

```python
import math
import jax
import jax.numpy as jnp
import numpy as np
from jax import lax

D = 3072
FF = 5376
TOP = 4
TOK_DEV = 64
EXPERTS = 8
CAP = 40
TOKENS = 512
N_EXPERT = 8


def level_of(own_key, extent, cuts, least, largest):
    def one(dim, shards_of):
        draws = jax.random.uniform(jax.random.fold_in(jax.random.fold_in(own_key, 6), dim), (shards_of,), jnp.float32, least / len(cuts), largest / len(cuts))
        return jnp.repeat(jnp.exp(draws), extent[dim] // shards_of).reshape((-1,) + (1,) * (len(extent) - dim - 1))

    factor_of = one(*cuts[0])
    for cut in cuts[1:]:
        factor_of = factor_of * one(*cut)
    return factor_of


def assign_block(rng, own, number, rows, amount, top, reach, slope):
    ranking = jax.random.permutation(rng, amount)
    crowded, common = shares(amount, rows * top, reach, slope, True), shares(amount, rows * top, reach, slope, False)
    places = jnp.arange(amount)

    def named(sizes, turn):
        used = int((sizes > 0).sum())
        fixed = max(1, used // 4)
        moved = fixed + (places - fixed + turn * (used - fixed)) % max(1, amount - fixed)
        return jnp.zeros((amount,), jnp.int32).at[ranking[jnp.where(places < fixed, places, moved)]].set(jnp.asarray(sizes, jnp.int32))

    sizes = jnp.where(number % 4 == 0, named(crowded, number // 4), named(common, number - number // 4 - 1))
    mixed = jax.random.permutation(jax.random.fold_in(own, 3), amount)
    giver, sink = mixed[0:amount // 2 * 2:2], mixed[1:amount // 2 * 2:2]
    slack = jnp.minimum(sizes[giver] - 1, reach - sizes[sink]) // 2
    slack = jnp.where((giver == ranking[0]) | (sink == ranking[0]) | (sizes[sink] == 0), 0, jnp.maximum(slack, 0))
    moved = jax.random.randint(jax.random.fold_in(own, 4), (amount // 2,), 0, 1 << 20) % (slack + 1)
    sizes = sizes.at[giver].add(-moved).at[sink].add(moved)
    labels = jnp.searchsorted(jnp.cumsum(sizes), jnp.arange(rows * top), side="right").astype(jnp.int32)
    table = labels.reshape(top, rows).T
    table = table[jax.random.permutation(jax.random.fold_in(own, 1), rows)]
    turn = jax.random.randint(jax.random.fold_in(own, 2), (rows, 1), 0, top)
    return jnp.take_along_axis(table, (jnp.arange(top)[None, :] + turn) % top, axis=1)


def shares(amount, total, reach, skew, full):
    loads = [(1 << 20) // math.isqrt(rank ** skew) + 1 for rank in range(1, amount + 1)]
    largest = reach if full else min(reach, max(-(-total // amount), total * loads[0] // sum(loads)))
    least = 1 if total - largest >= amount - 1 else 0
    given, surplus = [largest] + [least] * (amount - 1), total - largest - least * (amount - 1)
    while surplus > 0:
        candidates = [i for i in range(1, amount) if given[i] < largest] or [i for i in range(1, amount) if given[i] < reach]
        mass, left = sum([loads[i] for i in candidates]), surplus
        for i in candidates:
            addition = min(reach - given[i], max(1, left * loads[i] // mass), surplus)
            given[i] = given[i] + addition
            surplus = surplus - addition
    return np.array(given)


def bell_draw(rng, dims, deviation, most, shards=(), kind=jnp.bfloat16):
    level = level_of(rng, dims, shards, -0.22, 0.18) if shards else 1.0
    entries = jax.random.normal(rng, dims, jnp.float32) * deviation * level
    return jnp.minimum(jnp.maximum(entries, -most), most).astype(kind)


def setup_inputs(seed: int = 0) -> dict:
    streams_of = jax.random.split(jax.random.key(seed), 8)
    tokens = bell_draw(streams_of[0], (TOKENS, D), 1.0, 6.0, ((0, 8), (1, 4)))
    grad_out = bell_draw(streams_of[1], (TOKENS, D), 0.5, 3.0, ((0, 8), (1, 4)))
    probs = jnp.clip(jnp.exp(math.log(0.5) - 2.306499 * jax.random.uniform(streams_of[2], (TOKENS, TOP), jnp.float32) ** level_of(streams_of[2], (TOKENS, TOP), ((0, 8),), -0.2, 0.2)), 0.049804688, 0.5).astype(jnp.bfloat16)
    routes_keys = jax.random.split(jax.random.fold_in(streams_of[3], 1), TOKENS // TOK_DEV)
    routes_turns = jax.random.permutation(jax.random.fold_in(streams_of[3], 3), TOKENS // TOK_DEV)
    routes = jax.vmap(lambda own, number: assign_block(jax.random.fold_in(streams_of[3], 2), own, number, TOK_DEV, EXPERTS, TOP, CAP, 2))(routes_keys, routes_turns).reshape((TOKENS, TOP))
    gate_weight = bell_draw(streams_of[4], (EXPERTS, FF, D), D ** -0.5, 0.109375, ((0, 8), (1, 4)))
    up_weight = bell_draw(streams_of[5], (EXPERTS, FF, D), D ** -0.5, 0.109375, ((0, 8), (1, 4)))
    down_weight = bell_draw(streams_of[6], (EXPERTS, FF, D), FF ** -0.5, 0.078125, ((0, 8), (1, 4)))
    return dict(tokens=tokens, grad_out=grad_out, probs=probs, routes=routes, gate_weight=gate_weight, up_weight=up_weight, down_weight=down_weight)


def block_positions(flat_routes):
    experts_iota = jnp.arange(EXPERTS, dtype=jnp.int32)
    onehot = (flat_routes[:, None] == experts_iota[None, :]).astype(jnp.int32)
    before = jnp.cumsum(onehot, axis=0) - onehot
    return jnp.sum(before * onehot, axis=1).astype(jnp.int32)


def reference(tokens, grad_out, probs, routes, gate_weight, up_weight, down_weight):
    blocks = routes.reshape(N_EXPERT, TOK_DEV * TOP)
    position = jax.vmap(block_positions)(blocks)
    source = jnp.arange(N_EXPERT, dtype=jnp.int32)[:, None]
    row_index = (source * CAP + position).reshape(-1).astype(jnp.int32)
    expert_of = routes.reshape(-1).astype(jnp.int32)
    pair_ids = jnp.arange(TOKENS * TOP, dtype=jnp.int32)
    pair_table = jnp.full((EXPERTS, N_EXPERT * CAP), -1, dtype=jnp.int32)
    pair_table = pair_table.at[expert_of, row_index].set(pair_ids)
    flat_probs = probs.reshape(-1)

    def expert_grads(packed):
        pairs, w_gate, w_up, w_down = packed
        valid = pairs >= 0
        safe = jnp.where(valid, pairs, 0).astype(jnp.int32)
        token_ids = (safe // TOP).astype(jnp.int32)
        rows_x = jnp.where(valid[:, None], tokens[token_ids], 0).astype(jnp.bfloat16)
        rows_dy = jnp.where(valid[:, None], grad_out[token_ids], 0).astype(jnp.bfloat16)
        prob_rows = jnp.where(valid, flat_probs[safe].astype(jnp.float32), 0.0).astype(jnp.float32)
        pre_gate = jnp.dot(rows_x, w_gate.T, preferred_element_type=jnp.float32)
        pre_up = jnp.dot(rows_x, w_up.T, preferred_element_type=jnp.float32)
        sigmoid_a = jax.nn.sigmoid(pre_gate)
        silu_a = pre_gate * sigmoid_a
        hidden = (silu_a * pre_up).astype(jnp.bfloat16)
        back_hidden = jnp.dot(rows_dy, w_down.T, preferred_element_type=jnp.float32)
        scores = jnp.sum(hidden.astype(jnp.float32) * back_hidden, axis=1)
        scaled_hidden = (prob_rows[:, None] * hidden.astype(jnp.float32)).astype(jnp.bfloat16)
        down_grad = jnp.dot(scaled_hidden.T, rows_dy, preferred_element_type=jnp.float32).astype(jnp.bfloat16)
        hidden_grad = prob_rows[:, None] * back_hidden
        grad_gate = (hidden_grad * pre_up * sigmoid_a * (1.0 + pre_gate * (1.0 - sigmoid_a))).astype(jnp.bfloat16)
        grad_up = (hidden_grad * silu_a).astype(jnp.bfloat16)
        input_grad = jnp.dot(grad_gate, w_gate, preferred_element_type=jnp.float32) + jnp.dot(grad_up, w_up, preferred_element_type=jnp.float32)
        return input_grad, scores, down_grad

    input_grads, all_scores, d_down = lax.map(expert_grads, (pair_table, gate_weight, up_weight, down_weight))
    pairs_all = pair_table.reshape(-1)
    valid_all = pairs_all >= 0
    safe_all = jnp.where(valid_all, pairs_all, 0).astype(jnp.int32)
    token_all = (safe_all // TOP).astype(jnp.int32)
    grads_flat = jnp.where(valid_all[:, None], input_grads.reshape(-1, D), 0.0).astype(jnp.float32)
    d_tokens = jnp.zeros((TOKENS, D), jnp.float32).at[token_all].add(grads_flat).astype(jnp.bfloat16)
    scores_flat = jnp.where(valid_all, all_scores.reshape(-1), 0.0).astype(jnp.float32)
    d_probs = jnp.zeros((TOKENS * TOP,), jnp.float32).at[safe_all].add(scores_flat).reshape(TOKENS, TOP)
    return d_tokens, d_probs, d_down
```

```python
import functools

import jax
import jax.numpy as jnp
from jax import lax
from jax.experimental import pallas as pl
from jax.experimental.pallas import tpu as pltpu
from jax.sharding import PartitionSpec as P

TOK_DEV = 64
SLOTS = 320
MESH_ID = pl.DeviceIdType.MESH
VMEM = pltpu.VMEM


def greet(peers):
    barrier = pltpu.get_barrier_semaphore()
    for peer in peers:
        pl.semaphore_signal(barrier, inc=1, device_id=peer, device_id_type=MESH_ID)
    pl.semaphore_wait(barrier, len(peers))


def remote(src, dst, send_sem, recv_sem, peer):
    return pltpu.make_async_remote_copy(
        src_ref=src,
        dst_ref=dst,
        send_sem=send_sem,
        recv_sem=recv_sem,
        device_id=peer,
        device_id_type=MESH_ID,
    )


def flip(index, bit):
    if bit == 0:
        return index
    return index + bit - 2 * bit * lax.rem(index // bit, 2)


def flip_all(index, number):
    for bit in (1, 2, 4, 8):
        if number & bit:
            index = flip(index, bit)
    return index


def dispatch_kernel(
    n, send_ref, probs_ref, x_ref, dy_ref, got_probs_ref,
    rows, own_sem, out_send, out_recv, core_send, core_recv,
    side_send, side_recv, pass_send, pass_recv, prob_send, prob_recv,
):
    e = lax.axis_index("expert")
    t = lax.axis_index("tensor")
    width = send_ref.shape[2]
    cap = send_ref.shape[1] // 2
    core, side, far = flip(t, 1), flip(t, 2), flip(flip(t, 1), 2)
    others = [flip_all(e, j) for j in range(n)]
    greet([(o, t) for o in others[1:]] + [(e, core), (e, side)])

    def columns(index):
        return pl.ds(pl.multiple_of(index * width, 128), width)

    mine = [
        remote(send_ref.at[others[j]], rows.at[e, :, columns(t)], out_send.at[j], out_recv.at[j], (others[j], t))
        for j in range(1, n)
    ]
    small = [
        remote(probs_ref.at[others[j]], got_probs_ref.at[e], prob_send.at[j], prob_recv.at[j], (others[j], t))
        for j in range(1, n)
    ]
    own = pltpu.make_async_copy(send_ref.at[e], rows.at[e, :, columns(t)], own_sem.at[0])
    own_probs = pltpu.make_async_copy(probs_ref.at[e], got_probs_ref.at[e], own_sem.at[1])
    own.start()
    own_probs.start()
    for copy in mine:
        copy.start()
    for copy in small:
        copy.start()

    def block(j, index):
        return rows.at[others[j], :, columns(index)]

    to_core = [remote(block(j, t), block(j, t), core_send.at[j], core_recv.at[j], (e, core)) for j in range(n)]
    to_side = [remote(block(j, t), block(j, t), side_send.at[j], side_recv.at[j], (e, side)) for j in range(n)]
    passed = [remote(block(j, side), block(j, side), pass_send.at[j], pass_recv.at[j], (e, core)) for j in range(n)]
    lag = 2
    for j in range(n + lag):
        if j < n:
            if j == 0:
                own.wait()
            else:
                remote(send_ref.at[others[j]], block(j, t), out_send.at[j], out_recv.at[j], (others[j], t)).wait_recv()
            to_side[j].start()
            to_core[j].start()
        if j >= lag:
            k = j - lag
            remote(block(k, side), block(k, side), side_send.at[k], side_recv.at[k], (e, side)).wait_recv()
            passed[k].start()
    own_probs.wait()
    for j in range(1, n):
        remote(
            probs_ref.at[others[j]], got_probs_ref.at[others[j]], prob_send.at[j], prob_recv.at[j], (others[j], t)
        ).wait_recv()
    for j in range(n):
        remote(block(j, core), block(j, core), core_send.at[j], core_recv.at[j], (e, core)).wait_recv()
        remote(block(j, far), block(j, far), pass_send.at[j], pass_recv.at[j], (e, core)).wait_recv()
    for k in range(n // 2):
        for q in range(x_ref.shape[1] // width):
            cols = slice(q * width, (q + 1) * width)
            first = rows[2 * k, :, cols].astype(jnp.float32)
            second = rows[2 * k + 1, :, cols].astype(jnp.float32)
            span = slice(2 * k * cap, 2 * (k + 1) * cap)
            x_ref[span, cols] = jnp.concatenate([first[:cap], second[:cap]], axis=0).astype(jnp.bfloat16)
            dy_ref[span, cols] = jnp.concatenate([first[cap:], second[cap:]], axis=0).astype(jnp.bfloat16)
    for copy in mine + small + to_core + to_side + passed:
        copy.wait_send()


def dispatch(send, probs):
    n, double, width = send.shape
    tensor = lax.axis_size("tensor")
    slots = n * double // 2
    full = width * tensor
    dma = pltpu.SemaphoreType.DMA
    return pl.pallas_call(
        functools.partial(dispatch_kernel, n),
        out_shape=(
            jax.ShapeDtypeStruct((slots, full), jnp.bfloat16),
            jax.ShapeDtypeStruct((slots, full), jnp.bfloat16),
            jax.ShapeDtypeStruct(probs.shape, jnp.float32),
        ),
        in_specs=[pl.BlockSpec(memory_space=VMEM)] * 2,
        out_specs=[pl.BlockSpec(memory_space=VMEM)] * 3,
        scratch_shapes=[pltpu.VMEM((n, double, full), jnp.bfloat16), dma((2,))] + [dma((n,))] * 10,
        compiler_params=pltpu.CompilerParams(
            collective_id=0, has_side_effects=True, vmem_limit_bytes=40 * 1024 * 1024
        ),
        cost_estimate=pl.CostEstimate(flops=0, bytes_accessed=slots * full * 8, transcendentals=0),
    )(send, probs)


def combine_kernel(
    n, parts_ref, score_ref, got_ref, got_score_ref,
    from_core, mid, from_side, out, score_parts, score_sum,
    core_send, core_recv, side_send, side_recv, out_send, out_recv, own_sem,
    sum_send, sum_recv, score_send, score_recv,
):
    e = lax.axis_index("expert")
    t = lax.axis_index("tensor")
    core, side, far = flip(t, 1), flip(t, 2), flip(flip(t, 1), 2)
    others = [flip_all(e, j) for j in range(n)]
    chunk = mid.shape[1]
    chunks = mid.shape[0]
    cap = chunk // 2
    half = out.shape[2]
    greet([(o, t) for o in others[1:]] + [(e, core), (e, side), (e, far)])

    def span(k):
        return pl.ds(pl.multiple_of(k * chunk, chunk), chunk)

    order = [flip_all(e // 2, j) for j in range(chunks)]
    sums = [
        remote(score_ref, score_parts.at[i], sum_send.at[i], sum_recv.at[i], (e, peer))
        for i, peer in enumerate((core, side, far))
    ]
    to_core = []
    for j, k in enumerate(order):
        for i, quarter in enumerate((far, core)):
            to_core.append(
                remote(
                    parts_ref.at[quarter, span(k)], from_core.at[i, j],
                    core_send.at[i, j], core_recv.at[i, j], (e, core),
                )
            )
    for copy in to_core + sums:
        copy.start()
    to_side = []
    for j, k in enumerate(order):
        to_core[2 * j].wait_recv()
        mid[j] = (
            parts_ref[side, span(k), :].astype(jnp.float32) + from_core[0, j].astype(jnp.float32)
        ).astype(jnp.bfloat16)
        copy = remote(mid.at[j], from_side.at[j], side_send.at[j], side_recv.at[j], (e, side))
        copy.start()
        to_side.append(copy)
    for copy in sums:
        copy.wait_recv()
    score_sum[...] = score_ref[...] + score_parts[0] + score_parts[1] + score_parts[2]
    own_score = pltpu.make_async_copy(score_sum.at[e], got_score_ref.at[e], own_sem.at[1])
    own_score.start()
    sent = []
    for j in range(1, n):
        copy = remote(
            score_sum.at[others[j]], got_score_ref.at[e], score_send.at[j], score_recv.at[j], (others[j], t)
        )
        copy.start()
        sent.append(copy)
    own = pltpu.make_async_copy(out.at[0], got_ref.at[e], own_sem.at[0])
    for j, k in enumerate(order):
        to_core[2 * j + 1].wait_recv()
        to_side[j].wait_recv()
        total = (
            parts_ref[t, span(k), :].astype(jnp.float32)
            + from_core[1, j].astype(jnp.float32)
            + from_side[j].astype(jnp.float32)
        )
        low = jnp.concatenate([total[:cap, :half], total[:cap, half:]], axis=0).astype(jnp.bfloat16)
        high = jnp.concatenate([total[cap:, :half], total[cap:, half:]], axis=0).astype(jnp.bfloat16)
        odd = lax.rem(e, 2) == 1
        out[2 * j] = jnp.where(odd, high, low)
        out[2 * j + 1] = jnp.where(odd, low, high)
        for i in (2 * j, 2 * j + 1):
            if i == 0:
                own.start()
            else:
                copy = remote(out.at[i], got_ref.at[e], out_send.at[i], out_recv.at[i], (others[i], t))
                copy.start()
                sent.append(copy)
    own.wait()
    own_score.wait()
    for j in range(1, n):
        remote(out.at[j], got_ref.at[others[j]], out_send.at[j], out_recv.at[j], (others[j], t)).wait_recv()
        remote(
            score_sum.at[others[j]], got_score_ref.at[others[j]], score_send.at[j], score_recv.at[j], (others[j], t)
        ).wait_recv()
    for copy in to_core + sums + to_side + sent:
        copy.wait_send()


def combine(parts, scores):
    tensor, slots, width = parts.shape
    n = scores.shape[0]
    cap = slots // n
    chunk = 2 * cap
    dma = pltpu.SemaphoreType.DMA
    return pl.pallas_call(
        functools.partial(combine_kernel, n),
        out_shape=(
            jax.ShapeDtypeStruct((n, chunk, width // 2), jnp.bfloat16),
            jax.ShapeDtypeStruct(scores.shape, jnp.float32),
        ),
        in_specs=[pl.BlockSpec(memory_space=VMEM)] * 2,
        out_specs=[pl.BlockSpec(memory_space=VMEM)] * 2,
        scratch_shapes=[
            pltpu.VMEM((2, n // 2, chunk, width), jnp.bfloat16),
            pltpu.VMEM((n // 2, chunk, width), jnp.bfloat16),
            pltpu.VMEM((n // 2, chunk, width), jnp.bfloat16),
            pltpu.VMEM((n, chunk, width // 2), jnp.bfloat16),
            pltpu.VMEM((3,) + scores.shape, jnp.float32),
            pltpu.VMEM(scores.shape, jnp.float32),
            dma((2, n // 2)), dma((2, n // 2)),
            dma((n // 2,)), dma((n // 2,)),
            dma((n,)), dma((n,)), dma((2,)),
            dma((3,)), dma((3,)),
            dma((n,)), dma((n,)),
        ],
        compiler_params=pltpu.CompilerParams(
            collective_id=1, has_side_effects=True, vmem_limit_bytes=40 * 1024 * 1024
        ),
        cost_estimate=pl.CostEstimate(flops=0, bytes_accessed=slots * width * 8, transcendentals=0),
    )(parts, scores)


def expert_grads(rows_x, rows_dy, prob_rows, w_gate, w_up, w_down):
    slots = rows_x.shape[0]
    tensor = lax.axis_size("tensor")
    contract_last = (((1,), (1,)), ((), ()))
    pre_gate = lax.dot_general(rows_x, w_gate, contract_last, preferred_element_type=jnp.float32)
    pre_up = lax.dot_general(rows_x, w_up, contract_last, preferred_element_type=jnp.float32)
    sigmoid_a = jax.nn.sigmoid(pre_gate)
    silu_a = pre_gate * sigmoid_a
    hidden = (silu_a * pre_up).astype(jnp.bfloat16)
    back_hidden = lax.dot_general(rows_dy, w_down, contract_last, preferred_element_type=jnp.float32)
    score_part = jnp.sum(hidden.astype(jnp.float32) * back_hidden, axis=1)
    scaled_hidden = (prob_rows[:, None] * hidden.astype(jnp.float32)).astype(jnp.bfloat16)
    down_grad = lax.dot_general(
        scaled_hidden, rows_dy, (((0,), (0,)), ((), ())), preferred_element_type=jnp.float32
    ).astype(jnp.bfloat16)
    hidden_grad = prob_rows[:, None] * back_hidden
    grad_gate = (hidden_grad * pre_up * sigmoid_a * (1.0 + pre_gate * (1.0 - sigmoid_a))).astype(jnp.bfloat16)
    grad_up = (hidden_grad * silu_a).astype(jnp.bfloat16)
    input_grad = jnp.dot(grad_gate, w_gate, preferred_element_type=jnp.float32) + jnp.dot(
        grad_up, w_up, preferred_element_type=jnp.float32
    )
    parts = input_grad.astype(jnp.bfloat16).reshape(slots, tensor, -1).transpose(1, 0, 2)
    return parts, score_part, down_grad


def per_device(tokens, grad_out, probs, routes, gate_weight, up_weight, down_weight):
    n_experts = lax.axis_size("expert")
    capacity = min(SLOTS // n_experts, TOK_DEV)
    slots = n_experts * capacity
    tok_rows, width = tokens.shape
    half = width // 2
    top_count = routes.shape[1]
    flat_routes = routes.reshape(-1)
    pair_count = flat_routes.shape[0]
    experts_iota = lax.broadcasted_iota(jnp.int32, (pair_count, n_experts), 1)
    onehot = (flat_routes[:, None] == experts_iota).astype(jnp.int32)
    before = jnp.cumsum(onehot, axis=0) - onehot
    position = jnp.sum(before * onehot, axis=1)
    pair_slot = flat_routes * capacity + position
    slot_iota = lax.broadcasted_iota(jnp.int32, (slots, pair_count), 0)
    placer = (pair_slot[None, :] == slot_iota).astype(jnp.float32)
    token_placer = placer.reshape(slots, tok_rows, top_count).sum(axis=2)
    token_half = token_placer.astype(jnp.bfloat16)
    send_probs = jnp.sum(placer * probs.reshape(1, -1).astype(jnp.float32), axis=1)
    send_probs = jnp.broadcast_to(
        jnp.pad(send_probs.reshape(n_experts, 1, capacity), ((0, 0), (0, 0), (0, 128 - capacity))),
        (n_experts, 8, 128),
    )
    send_x = jnp.dot(token_half, tokens, preferred_element_type=jnp.float32).astype(jnp.bfloat16)
    send_dy = jnp.dot(token_half, grad_out, preferred_element_type=jnp.float32).astype(jnp.bfloat16)
    send = jnp.concatenate(
        [send_x.reshape(n_experts, capacity, width), send_dy.reshape(n_experts, capacity, width)], axis=1
    )
    rows_x, rows_dy, got_probs = dispatch(send, send_probs)
    prob_rows = got_probs[:, 0, :capacity].reshape(slots)
    parts, score_part, down_grad = expert_grads(
        rows_x, rows_dy, prob_rows, gate_weight[0], up_weight[0], down_weight[0]
    )
    score_block = jnp.broadcast_to(
        jnp.pad(score_part.reshape(n_experts, 1, capacity), ((0, 0), (0, 0), (0, 128 - capacity))),
        (n_experts, 8, 128),
    )
    back_rows, back_scores = combine(parts, score_block)
    back_rows = back_rows.reshape(n_experts, 2, capacity, half)
    token_grad = jnp.einsum(
        "est,ehsw->thw",
        token_half.reshape(n_experts, capacity, tok_rows),
        back_rows,
        preferred_element_type=jnp.float32,
    )
    d_tokens = token_grad.reshape(tok_rows, width).astype(jnp.bfloat16)
    scores = back_scores[:, 0, :capacity].reshape(slots, 1)
    d_probs = jnp.sum(placer * scores, axis=0).reshape(tok_rows, top_count)
    return d_tokens, d_probs, down_grad[None]


def plain_device(tokens, grad_out, probs, routes, gate_weight, up_weight, down_weight):
    n_experts = lax.axis_size("expert")
    capacity = min(SLOTS // n_experts, TOK_DEV)
    slots = n_experts * capacity
    tok_rows = routes.shape[0]
    top_count = routes.shape[1]
    flat_routes = routes.reshape(-1)
    pair_count = flat_routes.shape[0]
    experts_iota = lax.broadcasted_iota(jnp.int32, (pair_count, n_experts), 1)
    onehot = (flat_routes[:, None] == experts_iota).astype(jnp.int32)
    before = jnp.cumsum(onehot, axis=0) - onehot
    position = jnp.sum(before * onehot, axis=1)
    pair_slot = flat_routes * capacity + position
    slot_iota = lax.broadcasted_iota(jnp.int32, (slots, pair_count), 0)
    placer = (pair_slot[None, :] == slot_iota).astype(jnp.float32)
    token_placer = placer.reshape(slots, tok_rows, top_count).sum(axis=2)
    placer_half = placer.astype(jnp.bfloat16)
    token_half = token_placer.astype(jnp.bfloat16)
    send_probs = (
        jnp.dot(placer_half, probs.reshape(-1), preferred_element_type=jnp.float32)
        .astype(jnp.bfloat16)
        .reshape(n_experts, capacity)
    )
    send_x = (
        jnp.dot(token_half, tokens, preferred_element_type=jnp.float32)
        .astype(jnp.bfloat16)
        .reshape(n_experts, capacity, -1)
    )
    send_dy = (
        jnp.dot(token_half, grad_out, preferred_element_type=jnp.float32)
        .astype(jnp.bfloat16)
        .reshape(n_experts, capacity, -1)
    )
    got_x, got_dy, got_probs = (
        lax.all_to_all(send_x, "expert", split_axis=0, concat_axis=0, tiled=True),
        lax.all_to_all(send_dy, "expert", split_axis=0, concat_axis=0, tiled=True),
        lax.all_to_all(send_probs, "expert", split_axis=0, concat_axis=0, tiled=True),
    )
    rows_x, rows_dy = (
        lax.all_gather(got_x, "tensor", axis=2, tiled=True),
        lax.all_gather(got_dy, "tensor", axis=2, tiled=True),
    )
    rows_x = rows_x.reshape(slots, -1)
    rows_dy = rows_dy.reshape(slots, -1)
    prob_rows = got_probs.reshape(slots).astype(jnp.float32)
    w_gate = gate_weight[0]
    w_up = up_weight[0]
    w_down = down_weight[0]
    contract_last = (((1,), (1,)), ((), ()))
    pre_gate = lax.dot_general(rows_x, w_gate, contract_last, preferred_element_type=jnp.float32)
    pre_up = lax.dot_general(rows_x, w_up, contract_last, preferred_element_type=jnp.float32)
    sigmoid_a = jax.nn.sigmoid(pre_gate)
    silu_a = pre_gate * sigmoid_a
    hidden = (silu_a * pre_up).astype(jnp.bfloat16)
    back_hidden = lax.dot_general(
        rows_dy, w_down, contract_last, preferred_element_type=jnp.float32
    )
    score_part = jnp.sum(hidden.astype(jnp.float32) * back_hidden, axis=1)
    scaled_hidden = (prob_rows[:, None] * hidden.astype(jnp.float32)).astype(jnp.bfloat16)
    down_grad = lax.dot_general(
        scaled_hidden, rows_dy, (((0,), (0,)), ((), ())), preferred_element_type=jnp.float32
    ).astype(jnp.bfloat16)
    hidden_grad = prob_rows[:, None] * back_hidden
    grad_gate = (hidden_grad * pre_up * sigmoid_a * (1.0 + pre_gate * (1.0 - sigmoid_a))).astype(
        jnp.bfloat16
    )
    grad_up = (hidden_grad * silu_a).astype(jnp.bfloat16)
    input_grad = jnp.dot(grad_gate, w_gate, preferred_element_type=jnp.float32) + jnp.dot(
        grad_up, w_up, preferred_element_type=jnp.float32
    )
    scores = lax.psum(score_part, "tensor")
    score_block = scores.reshape(n_experts, capacity)
    grad_block = input_grad.reshape(n_experts, capacity, -1)
    placer_back = token_placer.T
    shares = lax.psum_scatter(grad_block, "tensor", scatter_dimension=2, tiled=True)
    back_rows, back_scores = (
        lax.all_to_all(shares, "expert", split_axis=0, concat_axis=0, tiled=True),
        lax.all_to_all(score_block, "expert", split_axis=0, concat_axis=0, tiled=True),
    )
    token_grad = jnp.dot(placer_back, back_rows.reshape(slots, -1), precision=lax.Precision.HIGHEST)
    d_tokens = token_grad.astype(jnp.bfloat16)
    d_probs = jnp.dot(
        placer.T, back_scores.reshape(slots), precision=lax.Precision.HIGHEST
    ).reshape(tok_rows, top_count)
    return (d_tokens, d_probs, down_grad[None])


def solution(mesh):
    regular = mesh.shape["tensor"] == 4 and mesh.shape["expert"] == 8
    return jax.shard_map(
        per_device if regular else plain_device,
        mesh=mesh,
        in_specs=(
            P("expert", "tensor"),
            P("expert", "tensor"),
            P("expert", None),
            P("expert", None),
            P("expert", "tensor", None),
            P("expert", "tensor", None),
            P("expert", "tensor", None),
        ),
        out_specs=(P("expert", "tensor"), P("expert", None), P("expert", "tensor", None)),
        check_vma=False,
    )
```

```python
import functools

import jax
import jax.numpy as jnp
from jax import lax
from jax.experimental import pallas as pl
from jax.experimental.pallas import tpu as pltpu
from jax.sharding import PartitionSpec as P

TOK_DEV = 64
SLOTS = 320
MESH_ID = pl.DeviceIdType.MESH
VMEM = pltpu.VMEM


def greet(peers):
    barrier = pltpu.get_barrier_semaphore()
    for peer in peers:
        pl.semaphore_signal(barrier, inc=1, device_id=peer, device_id_type=MESH_ID)
    pl.semaphore_wait(barrier, len(peers))


def remote(src, dst, send_sem, recv_sem, peer):
    return pltpu.make_async_remote_copy(
        src_ref=src,
        dst_ref=dst,
        send_sem=send_sem,
        recv_sem=recv_sem,
        device_id=peer,
        device_id_type=MESH_ID,
    )


def flip(index, bit):
    if bit == 0:
        return index
    return index + bit - 2 * bit * lax.rem(index // bit, 2)


def flip_all(index, number):
    for bit in (1, 2, 4, 8):
        if number & bit:
            index = flip(index, bit)
    return index


def dispatch_kernel(
    n, send_ref, probs_ref, x_ref, dy_ref, got_probs_ref,
    rows, own_sem, out_send, out_recv, core_send, core_recv,
    side_send, side_recv, pass_send, pass_recv, prob_send, prob_recv,
):
    e = lax.axis_index("expert")
    t = lax.axis_index("tensor")
    width = send_ref.shape[2]
    cap = send_ref.shape[1] // 2
    core, side, far = flip(t, 1), flip(t, 2), flip(flip(t, 1), 2)
    others = [flip_all(e, j) for j in range(n)]
    greet([(o, t) for o in others[1:]] + [(e, core), (e, side)])

    def columns(index):
        return pl.ds(pl.multiple_of(index * width, 128), width)

    mine = [
        remote(send_ref.at[others[j]], rows.at[e, :, columns(t)], out_send.at[j], out_recv.at[j], (others[j], t))
        for j in range(1, n)
    ]
    small = [
        remote(probs_ref.at[others[j]], got_probs_ref.at[e], prob_send.at[j], prob_recv.at[j], (others[j], t))
        for j in range(1, n)
    ]
    own = pltpu.make_async_copy(send_ref.at[e], rows.at[e, :, columns(t)], own_sem.at[0])
    own_probs = pltpu.make_async_copy(probs_ref.at[e], got_probs_ref.at[e], own_sem.at[1])
    own.start()
    own_probs.start()
    for copy in mine:
        copy.start()
    for copy in small:
        copy.start()

    def block(j, index):
        return rows.at[others[j], :, columns(index)]

    to_core = [remote(block(j, t), block(j, t), core_send.at[j], core_recv.at[j], (e, core)) for j in range(n)]
    to_side = [remote(block(j, t), block(j, t), side_send.at[j], side_recv.at[j], (e, side)) for j in range(n)]
    passed = [remote(block(j, side), block(j, side), pass_send.at[j], pass_recv.at[j], (e, core)) for j in range(n)]
    lag = 2
    for j in range(n + lag):
        if j < n:
            if j == 0:
                own.wait()
            else:
                remote(send_ref.at[others[j]], block(j, t), out_send.at[j], out_recv.at[j], (others[j], t)).wait_recv()
            to_side[j].start()
            to_core[j].start()
        if j >= lag:
            k = j - lag
            remote(block(k, side), block(k, side), side_send.at[k], side_recv.at[k], (e, side)).wait_recv()
            passed[k].start()
    own_probs.wait()
    for j in range(1, n):
        remote(
            probs_ref.at[others[j]], got_probs_ref.at[others[j]], prob_send.at[j], prob_recv.at[j], (others[j], t)
        ).wait_recv()
    for j in range(n):
        remote(block(j, core), block(j, core), core_send.at[j], core_recv.at[j], (e, core)).wait_recv()
        remote(block(j, far), block(j, far), pass_send.at[j], pass_recv.at[j], (e, core)).wait_recv()
    for k in range(n // 2):
        for q in range(x_ref.shape[1] // width):
            cols = slice(q * width, (q + 1) * width)
            first = rows[2 * k, :, cols].astype(jnp.float32)
            second = rows[2 * k + 1, :, cols].astype(jnp.float32)
            span = slice(2 * k * cap, 2 * (k + 1) * cap)
            x_ref[span, cols] = jnp.concatenate([first[:cap], second[:cap]], axis=0).astype(jnp.bfloat16)
            dy_ref[span, cols] = jnp.concatenate([first[cap:], second[cap:]], axis=0).astype(jnp.bfloat16)
    for copy in mine + small + to_core + to_side + passed:
        copy.wait_send()


def dispatch(send, probs):
    n, double, width = send.shape
    tensor = lax.axis_size("tensor")
    slots = n * double // 2
    full = width * tensor
    dma = pltpu.SemaphoreType.DMA
    return pl.pallas_call(
        functools.partial(dispatch_kernel, n),
        out_shape=(
            jax.ShapeDtypeStruct((slots, full), jnp.bfloat16),
            jax.ShapeDtypeStruct((slots, full), jnp.bfloat16),
            jax.ShapeDtypeStruct(probs.shape, jnp.float32),
        ),
        in_specs=[pl.BlockSpec(memory_space=VMEM)] * 2,
        out_specs=[pl.BlockSpec(memory_space=VMEM)] * 3,
        scratch_shapes=[pltpu.VMEM((n, double, full), jnp.bfloat16), dma((2,))] + [dma((n,))] * 10,
        compiler_params=pltpu.CompilerParams(
            collective_id=0, has_side_effects=True, vmem_limit_bytes=40 * 1024 * 1024
        ),
        cost_estimate=pl.CostEstimate(flops=0, bytes_accessed=slots * full * 8, transcendentals=0),
    )(send, probs)


def combine_kernel(
    n, gate_ref, up_ref, score_ref, w_gate, w_up, got_ref, got_score_ref,
    weights, keep, ship, from_core, mid, from_side, out, score_parts, score_sum,
    load_sem, core_send, core_recv, side_send, side_recv, out_send, out_recv, own_sem,
    sum_send, sum_recv, score_send, score_recv,
):
    e = lax.axis_index("expert")
    t = lax.axis_index("tensor")
    core, side, far = flip(t, 1), flip(t, 2), flip(flip(t, 1), 2)
    others = [flip_all(e, j) for j in range(n)]
    chunks, chunk, width = mid.shape
    cap = chunk // 2
    half = out.shape[2]
    quarters = (far, side, core, t)
    loads = []
    for i, quarter in enumerate(quarters):
        cols = pl.ds(pl.multiple_of(quarter * width, 128), width)
        for m, weight in enumerate((w_gate, w_up)):
            copy = pltpu.make_async_copy(weight.at[:, cols], weights.at[i, m], load_sem.at[i, m])
            copy.start()
            loads.append(copy)
    greet([(o, t) for o in others[1:]] + [(e, core), (e, side), (e, far)])
    sums = [
        remote(score_ref, score_parts.at[i], sum_send.at[i], sum_recv.at[i], (e, peer))
        for i, peer in enumerate((core, side, far))
    ]
    for copy in sums:
        copy.start()

    def product(i, dst):
        loads[2 * i].wait()
        loads[2 * i + 1].wait()

        @pl.loop(0, width // 256)
        def _(c):
            cols = pl.ds(pl.multiple_of(c * 256, 256), 256)
            dst[:, cols] = (
                jnp.dot(gate_ref[...], weights[i, 0, :, cols], preferred_element_type=jnp.float32)
                + jnp.dot(up_ref[...], weights[i, 1, :, cols], preferred_element_type=jnp.float32)
            ).astype(dst.dtype)

    def span(k):
        return pl.ds(pl.multiple_of(k * chunk, chunk), chunk)

    turns = (2, 3, 1, 0)
    pairs = [flip_all(e // 2, j) for j in range(chunks)]

    def give(i):
        copies = {}
        for j in turns:
            copies[j] = remote(
                ship.at[i, span(pairs[j])], from_core.at[i, j], core_send.at[i, j], core_recv.at[i, j], (e, core)
            )
            copies[j].start()
        return copies

    product(0, ship.at[0])
    give_far = give(0)
    product(1, keep.at[0])
    to_side = {}
    for j in turns:
        give_far[j].wait_recv()
        mid[j] = (keep[0, span(pairs[j]), :] + from_core[0, j].astype(jnp.float32)).astype(jnp.bfloat16)
        to_side[j] = remote(mid.at[j], from_side.at[j], side_send.at[j], side_recv.at[j], (e, side))
        to_side[j].start()
    product(2, ship.at[1])
    give_core = give(1)
    for copy in sums:
        copy.wait_recv()
    score_sum[...] = score_ref[...] + score_parts[0] + score_parts[1] + score_parts[2]
    own_score = pltpu.make_async_copy(score_sum.at[e], got_score_ref.at[e], own_sem.at[1])
    own_score.start()
    sent = []
    for j in range(1, n):
        copy = remote(
            score_sum.at[others[j]], got_score_ref.at[e], score_send.at[j], score_recv.at[j], (others[j], t)
        )
        copy.start()
        sent.append(copy)
    product(3, keep.at[1])
    own = pltpu.make_async_copy(out.at[0], got_ref.at[e], own_sem.at[0])
    for j in turns:
        give_core[j].wait_recv()
        to_side[j].wait_recv()
        total = (
            keep[1, span(pairs[j]), :] + from_core[1, j].astype(jnp.float32) + from_side[j].astype(jnp.float32)
        )
        low = jnp.concatenate([total[:cap, :half], total[:cap, half:]], axis=0).astype(jnp.bfloat16)
        high = jnp.concatenate([total[cap:, :half], total[cap:, half:]], axis=0).astype(jnp.bfloat16)
        odd = lax.rem(e, 2) == 1
        out[2 * j] = jnp.where(odd, high, low)
        out[2 * j + 1] = jnp.where(odd, low, high)
        for i in (2 * j, 2 * j + 1):
            if i == 0:
                own.start()
            else:
                copy = remote(out.at[i], got_ref.at[e], out_send.at[i], out_recv.at[i], (others[i], t))
                copy.start()
                sent.append(copy)
    own.wait()
    own_score.wait()
    for j in range(1, n):
        remote(out.at[j], got_ref.at[others[j]], out_send.at[j], out_recv.at[j], (others[j], t)).wait_recv()
        remote(
            score_sum.at[others[j]], got_score_ref.at[others[j]], score_send.at[j], score_recv.at[j], (others[j], t)
        ).wait_recv()
    for copy in list(give_far.values()) + list(give_core.values()) + sums + list(to_side.values()) + sent:
        copy.wait_send()


def combine(grad_gate, grad_up, scores, w_gate, w_up):
    tensor = lax.axis_size("tensor")
    slots, hidden = grad_gate.shape
    width = w_gate.shape[1] // tensor
    n = scores.shape[0]
    cap = slots // n
    chunk = 2 * cap
    dma = pltpu.SemaphoreType.DMA
    return pl.pallas_call(
        functools.partial(combine_kernel, n),
        out_shape=(
            jax.ShapeDtypeStruct((n, chunk, width // 2), jnp.bfloat16),
            jax.ShapeDtypeStruct(scores.shape, jnp.float32),
        ),
        in_specs=[pl.BlockSpec(memory_space=VMEM)] * 3 + [pl.BlockSpec(memory_space=pl.ANY)] * 2,
        out_specs=[pl.BlockSpec(memory_space=VMEM)] * 2,
        scratch_shapes=[
            pltpu.VMEM((tensor, 2, hidden, width), jnp.bfloat16),
            pltpu.VMEM((2, slots, width), jnp.float32),
            pltpu.VMEM((2, slots, width), jnp.bfloat16),
            pltpu.VMEM((2, n // 2, chunk, width), jnp.bfloat16),
            pltpu.VMEM((n // 2, chunk, width), jnp.bfloat16),
            pltpu.VMEM((n // 2, chunk, width), jnp.bfloat16),
            pltpu.VMEM((n, chunk, width // 2), jnp.bfloat16),
            pltpu.VMEM((3,) + scores.shape, jnp.float32),
            pltpu.VMEM(scores.shape, jnp.float32),
            dma((tensor, 2)),
            dma((2, n // 2)), dma((2, n // 2)),
            dma((n // 2,)), dma((n // 2,)),
            dma((n,)), dma((n,)), dma((2,)),
            dma((3,)), dma((3,)),
            dma((n,)), dma((n,)),
        ],
        compiler_params=pltpu.CompilerParams(
            collective_id=1, has_side_effects=True, vmem_limit_bytes=50 * 1024 * 1024
        ),
        cost_estimate=pl.CostEstimate(
            flops=4 * slots * hidden * width * tensor, bytes_accessed=4 * hidden * width * tensor, transcendentals=0
        ),
    )(grad_gate, grad_up, scores, w_gate, w_up)


def expert_grads(rows_x, rows_dy, prob_rows, w_gate, w_up, w_down):
    contract_last = (((1,), (1,)), ((), ()))
    pre_gate = lax.dot_general(rows_x, w_gate, contract_last, preferred_element_type=jnp.float32)
    pre_up = lax.dot_general(rows_x, w_up, contract_last, preferred_element_type=jnp.float32)
    sigmoid_a = jax.nn.sigmoid(pre_gate)
    silu_a = pre_gate * sigmoid_a
    hidden = (silu_a * pre_up).astype(jnp.bfloat16)
    back_hidden = lax.dot_general(rows_dy, w_down, contract_last, preferred_element_type=jnp.float32)
    score_part = jnp.sum(hidden.astype(jnp.float32) * back_hidden, axis=1)
    scaled_hidden = (prob_rows[:, None] * hidden.astype(jnp.float32)).astype(jnp.bfloat16)
    down_grad = lax.dot_general(
        scaled_hidden, rows_dy, (((0,), (0,)), ((), ())), preferred_element_type=jnp.float32
    ).astype(jnp.bfloat16)
    hidden_grad = prob_rows[:, None] * back_hidden
    grad_gate = (hidden_grad * pre_up * sigmoid_a * (1.0 + pre_gate * (1.0 - sigmoid_a))).astype(jnp.bfloat16)
    grad_up = (hidden_grad * silu_a).astype(jnp.bfloat16)
    return grad_gate, grad_up, score_part, down_grad


def per_device(tokens, grad_out, probs, routes, gate_weight, up_weight, down_weight):
    n_experts = lax.axis_size("expert")
    capacity = min(SLOTS // n_experts, TOK_DEV)
    slots = n_experts * capacity
    tok_rows, width = tokens.shape
    half = width // 2
    top_count = routes.shape[1]
    flat_routes = routes.reshape(-1)
    pair_count = flat_routes.shape[0]
    experts_iota = lax.broadcasted_iota(jnp.int32, (pair_count, n_experts), 1)
    onehot = (flat_routes[:, None] == experts_iota).astype(jnp.int32)
    before = jnp.cumsum(onehot, axis=0) - onehot
    position = jnp.sum(before * onehot, axis=1)
    pair_slot = flat_routes * capacity + position
    slot_iota = lax.broadcasted_iota(jnp.int32, (slots, pair_count), 0)
    placer = (pair_slot[None, :] == slot_iota).astype(jnp.float32)
    token_placer = placer.reshape(slots, tok_rows, top_count).sum(axis=2)
    token_half = token_placer.astype(jnp.bfloat16)
    send_probs = jnp.sum(placer * probs.reshape(1, -1).astype(jnp.float32), axis=1)
    send_probs = jnp.broadcast_to(
        jnp.pad(send_probs.reshape(n_experts, 1, capacity), ((0, 0), (0, 0), (0, 128 - capacity))),
        (n_experts, 8, 128),
    )
    send_x = jnp.dot(token_half, tokens, preferred_element_type=jnp.float32).astype(jnp.bfloat16)
    send_dy = jnp.dot(token_half, grad_out, preferred_element_type=jnp.float32).astype(jnp.bfloat16)
    send = jnp.concatenate(
        [send_x.reshape(n_experts, capacity, width), send_dy.reshape(n_experts, capacity, width)], axis=1
    )
    rows_x, rows_dy, got_probs = dispatch(send, send_probs)
    prob_rows = got_probs[:, 0, :capacity].reshape(slots)
    grad_gate, grad_up, score_part, down_grad = expert_grads(
        rows_x, rows_dy, prob_rows, gate_weight[0], up_weight[0], down_weight[0]
    )
    score_block = jnp.broadcast_to(
        jnp.pad(score_part.reshape(n_experts, 1, capacity), ((0, 0), (0, 0), (0, 128 - capacity))),
        (n_experts, 8, 128),
    )
    back_rows, back_scores = combine(grad_gate, grad_up, score_block, gate_weight[0], up_weight[0])
    back_rows = back_rows.reshape(n_experts, 2, capacity, half)
    token_grad = jnp.einsum(
        "est,ehsw->thw",
        token_half.reshape(n_experts, capacity, tok_rows),
        back_rows,
        preferred_element_type=jnp.float32,
    )
    d_tokens = token_grad.reshape(tok_rows, width).astype(jnp.bfloat16)
    scores = back_scores[:, 0, :capacity].reshape(slots, 1)
    d_probs = jnp.sum(placer * scores, axis=0).reshape(tok_rows, top_count)
    return d_tokens, d_probs, down_grad[None]


def plain_device(tokens, grad_out, probs, routes, gate_weight, up_weight, down_weight):
    n_experts = lax.axis_size("expert")
    capacity = min(SLOTS // n_experts, TOK_DEV)
    slots = n_experts * capacity
    tok_rows = routes.shape[0]
    top_count = routes.shape[1]
    flat_routes = routes.reshape(-1)
    pair_count = flat_routes.shape[0]
    experts_iota = lax.broadcasted_iota(jnp.int32, (pair_count, n_experts), 1)
    onehot = (flat_routes[:, None] == experts_iota).astype(jnp.int32)
    before = jnp.cumsum(onehot, axis=0) - onehot
    position = jnp.sum(before * onehot, axis=1)
    pair_slot = flat_routes * capacity + position
    slot_iota = lax.broadcasted_iota(jnp.int32, (slots, pair_count), 0)
    placer = (pair_slot[None, :] == slot_iota).astype(jnp.float32)
    token_placer = placer.reshape(slots, tok_rows, top_count).sum(axis=2)
    placer_half = placer.astype(jnp.bfloat16)
    token_half = token_placer.astype(jnp.bfloat16)
    send_probs = (
        jnp.dot(placer_half, probs.reshape(-1), preferred_element_type=jnp.float32)
        .astype(jnp.bfloat16)
        .reshape(n_experts, capacity)
    )
    send_x = (
        jnp.dot(token_half, tokens, preferred_element_type=jnp.float32)
        .astype(jnp.bfloat16)
        .reshape(n_experts, capacity, -1)
    )
    send_dy = (
        jnp.dot(token_half, grad_out, preferred_element_type=jnp.float32)
        .astype(jnp.bfloat16)
        .reshape(n_experts, capacity, -1)
    )
    got_x, got_dy, got_probs = (
        lax.all_to_all(send_x, "expert", split_axis=0, concat_axis=0, tiled=True),
        lax.all_to_all(send_dy, "expert", split_axis=0, concat_axis=0, tiled=True),
        lax.all_to_all(send_probs, "expert", split_axis=0, concat_axis=0, tiled=True),
    )
    rows_x, rows_dy = (
        lax.all_gather(got_x, "tensor", axis=2, tiled=True),
        lax.all_gather(got_dy, "tensor", axis=2, tiled=True),
    )
    rows_x = rows_x.reshape(slots, -1)
    rows_dy = rows_dy.reshape(slots, -1)
    prob_rows = got_probs.reshape(slots).astype(jnp.float32)
    w_gate = gate_weight[0]
    w_up = up_weight[0]
    w_down = down_weight[0]
    contract_last = (((1,), (1,)), ((), ()))
    pre_gate = lax.dot_general(rows_x, w_gate, contract_last, preferred_element_type=jnp.float32)
    pre_up = lax.dot_general(rows_x, w_up, contract_last, preferred_element_type=jnp.float32)
    sigmoid_a = jax.nn.sigmoid(pre_gate)
    silu_a = pre_gate * sigmoid_a
    hidden = (silu_a * pre_up).astype(jnp.bfloat16)
    back_hidden = lax.dot_general(
        rows_dy, w_down, contract_last, preferred_element_type=jnp.float32
    )
    score_part = jnp.sum(hidden.astype(jnp.float32) * back_hidden, axis=1)
    scaled_hidden = (prob_rows[:, None] * hidden.astype(jnp.float32)).astype(jnp.bfloat16)
    down_grad = lax.dot_general(
        scaled_hidden, rows_dy, (((0,), (0,)), ((), ())), preferred_element_type=jnp.float32
    ).astype(jnp.bfloat16)
    hidden_grad = prob_rows[:, None] * back_hidden
    grad_gate = (hidden_grad * pre_up * sigmoid_a * (1.0 + pre_gate * (1.0 - sigmoid_a))).astype(
        jnp.bfloat16
    )
    grad_up = (hidden_grad * silu_a).astype(jnp.bfloat16)
    input_grad = jnp.dot(grad_gate, w_gate, preferred_element_type=jnp.float32) + jnp.dot(
        grad_up, w_up, preferred_element_type=jnp.float32
    )
    scores = lax.psum(score_part, "tensor")
    score_block = scores.reshape(n_experts, capacity)
    grad_block = input_grad.reshape(n_experts, capacity, -1)
    placer_back = token_placer.T
    shares = lax.psum_scatter(grad_block, "tensor", scatter_dimension=2, tiled=True)
    back_rows, back_scores = (
        lax.all_to_all(shares, "expert", split_axis=0, concat_axis=0, tiled=True),
        lax.all_to_all(score_block, "expert", split_axis=0, concat_axis=0, tiled=True),
    )
    token_grad = jnp.dot(placer_back, back_rows.reshape(slots, -1), precision=lax.Precision.HIGHEST)
    d_tokens = token_grad.astype(jnp.bfloat16)
    d_probs = jnp.dot(
        placer.T, back_scores.reshape(slots), precision=lax.Precision.HIGHEST
    ).reshape(tok_rows, top_count)
    return (d_tokens, d_probs, down_grad[None])


def solution(mesh):
    regular = mesh.shape["tensor"] == 4 and mesh.shape["expert"] == 8
    return jax.shard_map(
        per_device if regular else plain_device,
        mesh=mesh,
        in_specs=(
            P("expert", "tensor"),
            P("expert", "tensor"),
            P("expert", None),
            P("expert", None),
            P("expert", "tensor", None),
            P("expert", "tensor", None),
            P("expert", "tensor", None),
        ),
        out_specs=(P("expert", "tensor"), P("expert", None), P("expert", "tensor", None)),
        check_vma=False,
    )
```

```python
import functools

import jax
import jax.numpy as jnp
from jax import lax
from jax.experimental import pallas as pl
from jax.experimental.pallas import tpu as pltpu
from jax.sharding import PartitionSpec as P

TOK_DEV = 64
SLOTS = 320
MESH_ID = pl.DeviceIdType.MESH
VMEM = pltpu.VMEM


def greet(peers):
    barrier = pltpu.get_barrier_semaphore()
    for peer in peers:
        pl.semaphore_signal(barrier, inc=1, device_id=peer, device_id_type=MESH_ID)
    pl.semaphore_wait(barrier, len(peers))


def remote(src, dst, send_sem, recv_sem, peer):
    return pltpu.make_async_remote_copy(
        src_ref=src,
        dst_ref=dst,
        send_sem=send_sem,
        recv_sem=recv_sem,
        device_id=peer,
        device_id_type=MESH_ID,
    )


def flip(index, bit):
    if bit == 0:
        return index
    return index + bit - 2 * bit * lax.rem(index // bit, 2)


def flip_all(index, number):
    for bit in (1, 2, 4, 8):
        if number & bit:
            index = flip(index, bit)
    return index


def dispatch_kernel(
    n, send_ref, probs_ref, w_gate, w_up, w_down, xy_ref, scaled_ref, gate_ref, up_ref, score_ref,
    rows, weights, acc, got_probs_ref, prob_rows, load_sem, own_sem, out_send, out_recv, core_send, core_recv,
    side_send, side_recv, pass_send, pass_recv, prob_send, prob_recv,
):
    e = lax.axis_index("expert")
    t = lax.axis_index("tensor")
    width = send_ref.shape[2]
    cap = send_ref.shape[1] // 2
    core, side, far = flip(t, 1), flip(t, 2), flip(flip(t, 1), 2)
    others = [flip_all(e, j) for j in range(n)]
    greet([(o, t) for o in others[1:]] + [(e, core), (e, side)])

    def columns(index):
        return pl.ds(pl.multiple_of(index * width, 128), width)

    mine = [
        remote(send_ref.at[others[j]], rows.at[e, :, columns(t)], out_send.at[j], out_recv.at[j], (others[j], t))
        for j in range(1, n)
    ]
    small = [
        remote(probs_ref.at[others[j]], got_probs_ref.at[e], prob_send.at[j], prob_recv.at[j], (others[j], t))
        for j in range(1, n)
    ]
    own = pltpu.make_async_copy(send_ref.at[e], rows.at[e, :, columns(t)], own_sem.at[0])
    own_probs = pltpu.make_async_copy(probs_ref.at[e], got_probs_ref.at[e], own_sem.at[1])
    own.start()
    own_probs.start()
    for copy in mine:
        copy.start()
    for copy in small:
        copy.start()
    loads = [
        pltpu.make_async_copy(weight, weights.at[m], load_sem.at[m]) for m, weight in enumerate((w_gate, w_up, w_down))
    ]
    for copy in loads:
        copy.start()

    def block(j, index):
        return rows.at[others[j], :, columns(index)]

    to_core = [remote(block(j, t), block(j, t), core_send.at[j], core_recv.at[j], (e, core)) for j in range(n)]
    to_side = [remote(block(j, t), block(j, t), side_send.at[j], side_recv.at[j], (e, side)) for j in range(n)]
    passed = [remote(block(j, side), block(j, side), pass_send.at[j], pass_recv.at[j], (e, core)) for j in range(n)]
    for j in range(n):
        if j == 0:
            own.wait()
        else:
            remote(send_ref.at[others[j]], block(j, t), out_send.at[j], out_recv.at[j], (others[j], t)).wait_recv()
        to_side[j].start()
        to_core[j].start()
    slots, full = xy_ref.shape[1:]
    hidden = gate_ref.shape[1]
    reach = 2 * width
    near = t // 2

    def half_columns(index):
        return pl.ds(pl.multiple_of(index * reach, 128), reach)

    def assemble(index):
        for c in range(2):
            cols = pl.ds(pl.multiple_of(index * reach + c * width, 128), width)

            for k in range(n // 2):
                first = rows[2 * k, :, cols].astype(jnp.float32)
                second = rows[2 * k + 1, :, cols].astype(jnp.float32)
                span = slice(2 * k * cap, 2 * (k + 1) * cap)
                xy_ref[0, span, cols] = jnp.concatenate([first[:cap], second[:cap]], axis=0).astype(jnp.bfloat16)
                xy_ref[1, span, cols] = jnp.concatenate([first[cap:], second[cap:]], axis=0).astype(jnp.bfloat16)

    def multiply(m, index, fresh):
        cols = half_columns(index)
        for low in range(0, hidden, 512):
            tile = slice(low, min(low + 512, hidden))
            part = lax.dot_general(
                xy_ref[m // 2, :, cols],
                weights[m, tile, cols],
                (((1,), (1,)), ((), ())),
                preferred_element_type=jnp.float32,
            )
            acc[m, :, tile] = part if fresh else acc[m, :, tile] + part

    def pass_on(k):
        remote(block(k, side), block(k, side), side_send.at[k], side_recv.at[k], (e, side)).wait_recv()
        passed[k].start()

    for k in range(n // 2):
        pass_on(k)
    for j in range(n):
        remote(block(j, core), block(j, core), core_send.at[j], core_recv.at[j], (e, core)).wait_recv()
    assemble(near)
    for m in range(3):
        loads[m].wait()
        multiply(m, near, True)
        if m < 2:
            pass_on(n // 2 + m)
    for k in range(n // 2 + 2, n):
        pass_on(k)
    own_probs.wait()
    for j in range(1, n):
        remote(
            probs_ref.at[others[j]], got_probs_ref.at[others[j]], prob_send.at[j], prob_recv.at[j], (others[j], t)
        ).wait_recv()
    for s in range(n):
        prob_rows[s * cap : (s + 1) * cap, :] = got_probs_ref[s]
    for j in range(n):
        remote(block(j, far), block(j, far), pass_send.at[j], pass_recv.at[j], (e, core)).wait_recv()
    assemble(1 - near)
    for m in range(3):
        multiply(m, 1 - near, False)

    @pl.loop(0, slots // 16)
    def _(r):
        span = pl.ds(pl.multiple_of(r * 16, 16), 16)
        prob = prob_rows[span, 0:1]
        score = jnp.zeros((16, 1), jnp.float32)
        for low in range(0, hidden, 384):
            tile = slice(low, min(low + 384, hidden))
            pre_gate = acc[0, span, tile]
            pre_up = acc[1, span, tile]
            back = acc[2, span, tile]
            sigmoid = jax.nn.sigmoid(pre_gate)
            silu = pre_gate * sigmoid
            hid = (silu * pre_up).astype(jnp.bfloat16).astype(jnp.float32)
            score = score + jnp.sum(hid * back, axis=1, keepdims=True)
            scaled_ref[span, tile] = (prob * hid).astype(jnp.bfloat16)
            grad = prob * back
            gate_ref[span, tile] = (grad * pre_up * sigmoid * (1.0 + pre_gate * (1.0 - sigmoid))).astype(jnp.bfloat16)
            up_ref[span, tile] = (grad * silu).astype(jnp.bfloat16)
        score_ref[span, :] = jnp.broadcast_to(score, (16, 128))

    for copy in mine + small + to_core + to_side + passed:
        copy.wait_send()


def dispatch(send, probs, w_gate, w_up, w_down):
    n, double, width = send.shape
    cap = double // 2
    slots = n * cap
    hidden, full = w_gate.shape
    dma = pltpu.SemaphoreType.DMA
    small = jax.ShapeDtypeStruct((slots, hidden), jnp.bfloat16)
    return pl.pallas_call(
        functools.partial(dispatch_kernel, n),
        out_shape=(
            jax.ShapeDtypeStruct((2, slots, full), jnp.bfloat16),
            small,
            small,
            small,
            jax.ShapeDtypeStruct((slots, 128), jnp.float32),
        ),
        in_specs=[pl.BlockSpec(memory_space=VMEM)] * 2 + [pl.BlockSpec(memory_space=pl.ANY)] * 3,
        out_specs=[pl.BlockSpec(memory_space=VMEM)] * 5,
        scratch_shapes=[
            pltpu.VMEM((n, double, full), jnp.bfloat16),
            pltpu.VMEM((3, hidden, full), jnp.bfloat16),
            pltpu.VMEM((3, slots, hidden), jnp.float32),
            pltpu.VMEM((n, cap, 128), jnp.float32),
            pltpu.VMEM((slots, 128), jnp.float32),
            dma((3,)),
            dma((2,)),
        ]
        + [dma((n,))] * 10,
        compiler_params=pltpu.CompilerParams(
            collective_id=0, has_side_effects=True, vmem_limit_bytes=54 * 1024 * 1024
        ),
        cost_estimate=pl.CostEstimate(
            flops=6 * slots * full * hidden, bytes_accessed=6 * hidden * full, transcendentals=slots * hidden
        ),
    )(send, probs, w_gate, w_up, w_down)


def combine_kernel(
    n, gate_ref, up_ref, scaled_ref, xy_ref, score_ref, w_gate, w_up, got_ref, got_score_ref, down_ref,
    weights, keep, ship, from_core, mid, from_side, out, score_parts, score_sum,
    load_sem, core_send, core_recv, side_send, side_recv, out_send, out_recv, own_sem,
    sum_send, sum_recv, score_send, score_recv,
):
    e = lax.axis_index("expert")
    t = lax.axis_index("tensor")
    core, side, far = flip(t, 1), flip(t, 2), flip(flip(t, 1), 2)
    others = [flip_all(e, j) for j in range(n)]
    chunks, chunk, width = mid.shape
    cap = chunk // 2
    half = out.shape[2]
    quarters = (far, side, core, t)
    loads = []
    for i, quarter in enumerate(quarters):
        cols = pl.ds(pl.multiple_of(quarter * width, 128), width)
        for m, weight in enumerate((w_gate, w_up)):
            copy = pltpu.make_async_copy(weight.at[:, cols], weights.at[i, m], load_sem.at[i, m])
            copy.start()
            loads.append(copy)
    greet([(o, t) for o in others[1:]] + [(e, core), (e, side), (e, far)])
    sums = [
        remote(score_ref, score_parts.at[i], sum_send.at[i], sum_recv.at[i], (e, peer))
        for i, peer in enumerate((core, side, far))
    ]
    for copy in sums:
        copy.start()

    def product(i, dst):
        loads[2 * i].wait()
        loads[2 * i + 1].wait()

        @pl.loop(0, width // 256)
        def _(c):
            cols = pl.ds(pl.multiple_of(c * 256, 256), 256)
            dst[:, cols] = (
                jnp.dot(gate_ref[...], weights[i, 0, :, cols], preferred_element_type=jnp.float32)
                + jnp.dot(up_ref[...], weights[i, 1, :, cols], preferred_element_type=jnp.float32)
            ).astype(dst.dtype)

    def span(k):
        return pl.ds(pl.multiple_of(k * chunk, chunk), chunk)

    def down_tile(low):
        cols = slice(low, low + 256)
        down_ref[:, cols] = lax.dot_general(
            scaled_ref[...], xy_ref[1, :, cols], (((0,), (0,)), ((), ())), preferred_element_type=jnp.float32
        ).astype(jnp.bfloat16)

    down_lows = list(range(0, down_ref.shape[1], 256))
    turns = (2, 3, 1, 0)
    pairs = [flip_all(e // 2, j) for j in range(chunks)]

    def give(i):
        copies = {}
        for j in turns:
            copies[j] = remote(
                ship.at[i, span(pairs[j])], from_core.at[i, j], core_send.at[i, j], core_recv.at[i, j], (e, core)
            )
            copies[j].start()
        return copies

    product(0, ship.at[0])
    give_far = give(0)
    product(1, keep.at[0])
    to_side = {}
    for j in turns:
        give_far[j].wait_recv()
        mid[j] = (keep[0, span(pairs[j]), :] + from_core[0, j].astype(jnp.float32)).astype(jnp.bfloat16)
        to_side[j] = remote(mid.at[j], from_side.at[j], side_send.at[j], side_recv.at[j], (e, side))
        to_side[j].start()
    product(2, ship.at[1])
    give_core = give(1)
    for copy in sums:
        copy.wait_recv()
    score_sum[...] = score_ref[...] + score_parts[0] + score_parts[1] + score_parts[2]
    own_score = pltpu.make_async_copy(score_sum.at[e], got_score_ref.at[e], own_sem.at[1])
    own_score.start()
    sent = []
    for j in range(1, n):
        copy = remote(
            score_sum.at[others[j]], got_score_ref.at[e], score_send.at[j], score_recv.at[j], (others[j], t)
        )
        copy.start()
        sent.append(copy)
    product(3, keep.at[1])
    own = pltpu.make_async_copy(out.at[0], got_ref.at[e], own_sem.at[0])
    for j in turns:
        down_tile(down_lows.pop())
        give_core[j].wait_recv()
        to_side[j].wait_recv()
        total = (
            keep[1, span(pairs[j]), :] + from_core[1, j].astype(jnp.float32) + from_side[j].astype(jnp.float32)
        )
        low = jnp.concatenate([total[:cap, :half], total[:cap, half:]], axis=0).astype(jnp.bfloat16)
        high = jnp.concatenate([total[cap:, :half], total[cap:, half:]], axis=0).astype(jnp.bfloat16)
        odd = lax.rem(e, 2) == 1
        out[2 * j] = jnp.where(odd, high, low)
        out[2 * j + 1] = jnp.where(odd, low, high)
        for i in (2 * j, 2 * j + 1):
            if i == 0:
                own.start()
            else:
                copy = remote(out.at[i], got_ref.at[e], out_send.at[i], out_recv.at[i], (others[i], t))
                copy.start()
                sent.append(copy)
    for low in down_lows:
        down_tile(low)
    own.wait()
    own_score.wait()
    for j in range(1, n):
        remote(out.at[j], got_ref.at[others[j]], out_send.at[j], out_recv.at[j], (others[j], t)).wait_recv()
        remote(
            score_sum.at[others[j]], got_score_ref.at[others[j]], score_send.at[j], score_recv.at[j], (others[j], t)
        ).wait_recv()
    for copy in list(give_far.values()) + list(give_core.values()) + sums + list(to_side.values()) + sent:
        copy.wait_send()


def combine(grad_gate, grad_up, scaled, xy, scores, w_gate, w_up):
    tensor = lax.axis_size("tensor")
    slots, hidden = grad_gate.shape
    width = w_gate.shape[1] // tensor
    n = scores.shape[0]
    cap = slots // n
    chunk = 2 * cap
    dma = pltpu.SemaphoreType.DMA
    return pl.pallas_call(
        functools.partial(combine_kernel, n),
        out_shape=(
            jax.ShapeDtypeStruct((n, chunk, width // 2), jnp.bfloat16),
            jax.ShapeDtypeStruct(scores.shape, jnp.float32),
            jax.ShapeDtypeStruct(w_gate.shape, jnp.bfloat16),
        ),
        in_specs=[pl.BlockSpec(memory_space=VMEM)] * 5 + [pl.BlockSpec(memory_space=pl.ANY)] * 2,
        out_specs=[pl.BlockSpec(memory_space=VMEM)] * 3,
        scratch_shapes=[
            pltpu.VMEM((tensor, 2, hidden, width), jnp.bfloat16),
            pltpu.VMEM((2, slots, width), jnp.float32),
            pltpu.VMEM((2, slots, width), jnp.bfloat16),
            pltpu.VMEM((2, n // 2, chunk, width), jnp.bfloat16),
            pltpu.VMEM((n // 2, chunk, width), jnp.bfloat16),
            pltpu.VMEM((n // 2, chunk, width), jnp.bfloat16),
            pltpu.VMEM((n, chunk, width // 2), jnp.bfloat16),
            pltpu.VMEM((3,) + scores.shape, jnp.float32),
            pltpu.VMEM(scores.shape, jnp.float32),
            dma((tensor, 2)),
            dma((2, n // 2)), dma((2, n // 2)),
            dma((n // 2,)), dma((n // 2,)),
            dma((n,)), dma((n,)), dma((2,)),
            dma((3,)), dma((3,)),
            dma((n,)), dma((n,)),
        ],
        compiler_params=pltpu.CompilerParams(
            collective_id=1, has_side_effects=True, vmem_limit_bytes=54 * 1024 * 1024
        ),
        cost_estimate=pl.CostEstimate(
            flops=4 * slots * hidden * width * tensor, bytes_accessed=4 * hidden * width * tensor, transcendentals=0
        ),
    )(grad_gate, grad_up, scaled, xy, scores, w_gate, w_up)


def per_device(tokens, grad_out, probs, routes, gate_weight, up_weight, down_weight):
    n_experts = lax.axis_size("expert")
    capacity = min(SLOTS // n_experts, TOK_DEV)
    slots = n_experts * capacity
    tok_rows, width = tokens.shape
    half = width // 2
    top_count = routes.shape[1]
    flat_routes = routes.reshape(-1)
    pair_count = flat_routes.shape[0]
    experts_iota = lax.broadcasted_iota(jnp.int32, (pair_count, n_experts), 1)
    onehot = (flat_routes[:, None] == experts_iota).astype(jnp.int32)
    before = jnp.cumsum(onehot, axis=0) - onehot
    position = jnp.sum(before * onehot, axis=1)
    pair_slot = flat_routes * capacity + position
    slot_iota = lax.broadcasted_iota(jnp.int32, (slots, pair_count), 0)
    placer = (pair_slot[None, :] == slot_iota).astype(jnp.float32)
    token_placer = placer.reshape(slots, tok_rows, top_count).sum(axis=2)
    token_half = token_placer.astype(jnp.bfloat16)
    send_probs = jnp.sum(placer * probs.reshape(1, -1).astype(jnp.float32), axis=1)
    send_probs = jnp.broadcast_to(send_probs.reshape(n_experts, capacity, 1), (n_experts, capacity, 128))
    send_x = jnp.dot(token_half, tokens, preferred_element_type=jnp.float32).astype(jnp.bfloat16)
    send_dy = jnp.dot(token_half, grad_out, preferred_element_type=jnp.float32).astype(jnp.bfloat16)
    send = jnp.concatenate(
        [send_x.reshape(n_experts, capacity, width), send_dy.reshape(n_experts, capacity, width)], axis=1
    )
    xy, scaled, grad_gate, grad_up, score_part = dispatch(
        send, send_probs, gate_weight[0], up_weight[0], down_weight[0]
    )
    score_part = score_part[:, 0]
    score_block = jnp.broadcast_to(
        jnp.pad(score_part.reshape(n_experts, 1, capacity), ((0, 0), (0, 0), (0, 128 - capacity))),
        (n_experts, 8, 128),
    )
    back_rows, back_scores, down_grad = combine(
        grad_gate, grad_up, scaled, xy, score_block, gate_weight[0], up_weight[0]
    )
    back_rows = back_rows.reshape(n_experts, 2, capacity, half)
    token_grad = jnp.einsum(
        "est,ehsw->thw",
        token_half.reshape(n_experts, capacity, tok_rows),
        back_rows,
        preferred_element_type=jnp.float32,
    )
    d_tokens = token_grad.reshape(tok_rows, width).astype(jnp.bfloat16)
    scores = back_scores[:, 0, :capacity].reshape(slots, 1)
    d_probs = jnp.sum(placer * scores, axis=0).reshape(tok_rows, top_count)
    return d_tokens, d_probs, down_grad[None]


def plain_device(tokens, grad_out, probs, routes, gate_weight, up_weight, down_weight):
    n_experts = lax.axis_size("expert")
    capacity = min(SLOTS // n_experts, TOK_DEV)
    slots = n_experts * capacity
    tok_rows = routes.shape[0]
    top_count = routes.shape[1]
    flat_routes = routes.reshape(-1)
    pair_count = flat_routes.shape[0]
    experts_iota = lax.broadcasted_iota(jnp.int32, (pair_count, n_experts), 1)
    onehot = (flat_routes[:, None] == experts_iota).astype(jnp.int32)
    before = jnp.cumsum(onehot, axis=0) - onehot
    position = jnp.sum(before * onehot, axis=1)
    pair_slot = flat_routes * capacity + position
    slot_iota = lax.broadcasted_iota(jnp.int32, (slots, pair_count), 0)
    placer = (pair_slot[None, :] == slot_iota).astype(jnp.float32)
    token_placer = placer.reshape(slots, tok_rows, top_count).sum(axis=2)
    placer_half = placer.astype(jnp.bfloat16)
    token_half = token_placer.astype(jnp.bfloat16)
    send_probs = (
        jnp.dot(placer_half, probs.reshape(-1), preferred_element_type=jnp.float32)
        .astype(jnp.bfloat16)
        .reshape(n_experts, capacity)
    )
    send_x = (
        jnp.dot(token_half, tokens, preferred_element_type=jnp.float32)
        .astype(jnp.bfloat16)
        .reshape(n_experts, capacity, -1)
    )
    send_dy = (
        jnp.dot(token_half, grad_out, preferred_element_type=jnp.float32)
        .astype(jnp.bfloat16)
        .reshape(n_experts, capacity, -1)
    )
    got_x, got_dy, got_probs = (
        lax.all_to_all(send_x, "expert", split_axis=0, concat_axis=0, tiled=True),
        lax.all_to_all(send_dy, "expert", split_axis=0, concat_axis=0, tiled=True),
        lax.all_to_all(send_probs, "expert", split_axis=0, concat_axis=0, tiled=True),
    )
    rows_x, rows_dy = (
        lax.all_gather(got_x, "tensor", axis=2, tiled=True),
        lax.all_gather(got_dy, "tensor", axis=2, tiled=True),
    )
    rows_x = rows_x.reshape(slots, -1)
    rows_dy = rows_dy.reshape(slots, -1)
    prob_rows = got_probs.reshape(slots).astype(jnp.float32)
    w_gate = gate_weight[0]
    w_up = up_weight[0]
    w_down = down_weight[0]
    contract_last = (((1,), (1,)), ((), ()))
    pre_gate = lax.dot_general(rows_x, w_gate, contract_last, preferred_element_type=jnp.float32)
    pre_up = lax.dot_general(rows_x, w_up, contract_last, preferred_element_type=jnp.float32)
    sigmoid_a = jax.nn.sigmoid(pre_gate)
    silu_a = pre_gate * sigmoid_a
    hidden = (silu_a * pre_up).astype(jnp.bfloat16)
    back_hidden = lax.dot_general(
        rows_dy, w_down, contract_last, preferred_element_type=jnp.float32
    )
    score_part = jnp.sum(hidden.astype(jnp.float32) * back_hidden, axis=1)
    scaled_hidden = (prob_rows[:, None] * hidden.astype(jnp.float32)).astype(jnp.bfloat16)
    down_grad = lax.dot_general(
        scaled_hidden, rows_dy, (((0,), (0,)), ((), ())), preferred_element_type=jnp.float32
    ).astype(jnp.bfloat16)
    hidden_grad = prob_rows[:, None] * back_hidden
    grad_gate = (hidden_grad * pre_up * sigmoid_a * (1.0 + pre_gate * (1.0 - sigmoid_a))).astype(
        jnp.bfloat16
    )
    grad_up = (hidden_grad * silu_a).astype(jnp.bfloat16)
    input_grad = jnp.dot(grad_gate, w_gate, preferred_element_type=jnp.float32) + jnp.dot(
        grad_up, w_up, preferred_element_type=jnp.float32
    )
    scores = lax.psum(score_part, "tensor")
    score_block = scores.reshape(n_experts, capacity)
    grad_block = input_grad.reshape(n_experts, capacity, -1)
    placer_back = token_placer.T
    shares = lax.psum_scatter(grad_block, "tensor", scatter_dimension=2, tiled=True)
    back_rows, back_scores = (
        lax.all_to_all(shares, "expert", split_axis=0, concat_axis=0, tiled=True),
        lax.all_to_all(score_block, "expert", split_axis=0, concat_axis=0, tiled=True),
    )
    token_grad = jnp.dot(placer_back, back_rows.reshape(slots, -1), precision=lax.Precision.HIGHEST)
    d_tokens = token_grad.astype(jnp.bfloat16)
    d_probs = jnp.dot(
        placer.T, back_scores.reshape(slots), precision=lax.Precision.HIGHEST
    ).reshape(tok_rows, top_count)
    return (d_tokens, d_probs, down_grad[None])


def solution(mesh):
    regular = mesh.shape["tensor"] == 4 and mesh.shape["expert"] == 8
    return jax.shard_map(
        per_device if regular else plain_device,
        mesh=mesh,
        in_specs=(
            P("expert", "tensor"),
            P("expert", "tensor"),
            P("expert", None),
            P("expert", None),
            P("expert", "tensor", None),
            P("expert", "tensor", None),
            P("expert", "tensor", None),
        ),
        out_specs=(P("expert", "tensor"), P("expert", None), P("expert", "tensor", None)),
        check_vma=False,
    )
```

```python
import functools

import jax
import jax.numpy as jnp
from jax import lax
from jax.experimental import pallas as pl
from jax.experimental.pallas import tpu as pltpu
from jax.sharding import PartitionSpec as P

TOK_DEV = 64
SLOTS = 320
MESH_ID = pl.DeviceIdType.MESH
VMEM = pltpu.VMEM


def greet(peers):
    barrier = pltpu.get_barrier_semaphore()
    for peer in peers:
        pl.semaphore_signal(barrier, inc=1, device_id=peer, device_id_type=MESH_ID)
    pl.semaphore_wait(barrier, len(peers))


def remote(src, dst, send_sem, recv_sem, peer):
    return pltpu.make_async_remote_copy(
        src_ref=src,
        dst_ref=dst,
        send_sem=send_sem,
        recv_sem=recv_sem,
        device_id=peer,
        device_id_type=MESH_ID,
    )


def flip(index, bit):
    if bit == 0:
        return index
    return index + bit - 2 * bit * lax.rem(index // bit, 2)


def flip_all(index, number):
    for bit in (1, 2, 4, 8):
        if number & bit:
            index = flip(index, bit)
    return index


def dispatch_kernel(
    n, send_ref, probs_ref, w_gate, w_up, w_down, dy_ref, scaled_ref, gate_ref, up_ref, score_ref,
    rows, weights, acc, x_rows, score_rows, got_probs_ref, prob_rows, load_sem, own_sem, out_send, out_recv, core_send, core_recv,
    side_send, side_recv, pass_send, pass_recv, prob_send, prob_recv,
):
    e = lax.axis_index("expert")
    t = lax.axis_index("tensor")
    width = send_ref.shape[2]
    cap = send_ref.shape[1] // 2
    core, side, far = flip(t, 1), flip(t, 2), flip(flip(t, 1), 2)
    others = [flip_all(e, j) for j in range(n)]
    greet([(o, t) for o in others[1:]] + [(e, core), (e, side)])

    def columns(index):
        return pl.ds(pl.multiple_of(index * width, 128), width)

    mine = [
        remote(send_ref.at[others[j]], rows.at[e, :, columns(t)], out_send.at[j], out_recv.at[j], (others[j], t))
        for j in range(1, n)
    ]
    small = [
        remote(probs_ref.at[others[j]], got_probs_ref.at[e], prob_send.at[j], prob_recv.at[j], (others[j], t))
        for j in range(1, n)
    ]
    own = pltpu.make_async_copy(send_ref.at[e], rows.at[e, :, columns(t)], own_sem.at[0])
    own_probs = pltpu.make_async_copy(probs_ref.at[e], got_probs_ref.at[e], own_sem.at[1])
    own.start()
    own_probs.start()
    for copy in mine:
        copy.start()
    for copy in small:
        copy.start()
    loads = [
        pltpu.make_async_copy(weight, weights.at[m], load_sem.at[m]) for m, weight in enumerate((w_gate, w_up, w_down))
    ]
    for copy in loads:
        copy.start()

    def block(j, index):
        return rows.at[others[j], :, columns(index)]

    to_core = [remote(block(j, t), block(j, t), core_send.at[j], core_recv.at[j], (e, core)) for j in range(n)]
    to_side = [remote(block(j, t), block(j, t), side_send.at[j], side_recv.at[j], (e, side)) for j in range(n)]
    passed = [remote(block(j, side), block(j, side), pass_send.at[j], pass_recv.at[j], (e, core)) for j in range(n)]
    for j in range(n):
        if j == 0:
            own.wait()
        else:
            remote(send_ref.at[others[j]], block(j, t), out_send.at[j], out_recv.at[j], (others[j], t)).wait_recv()
        to_side[j].start()
        to_core[j].start()
    slots = dy_ref.shape[0]
    hidden = gate_ref.shape[1]
    reach = 2 * width
    near = t // 2

    def half_columns(index):
        return pl.ds(pl.multiple_of(index * reach, 128), reach)

    def assemble(index):
        for c in range(2):
            cols = pl.ds(pl.multiple_of(index * reach + c * width, 128), width)

            for k in range(n // 2):
                first = rows[2 * k, :, cols].astype(jnp.float32)
                second = rows[2 * k + 1, :, cols].astype(jnp.float32)
                span = slice(2 * k * cap, 2 * (k + 1) * cap)
                x_rows[span, cols] = jnp.concatenate([first[:cap], second[:cap]], axis=0).astype(jnp.bfloat16)
                dy_ref[span, cols] = jnp.concatenate([first[cap:], second[cap:]], axis=0).astype(jnp.bfloat16)

    def multiply(m, index, fresh):
        cols = half_columns(index)
        for low in range(0, hidden, 512):
            tile = slice(low, min(low + 512, hidden))
            part = lax.dot_general(
                (dy_ref if m == 2 else x_rows)[:, cols],
                weights[m, tile, cols],
                (((1,), (1,)), ((), ())),
                preferred_element_type=jnp.float32,
            )
            acc[m, :, tile] = part if fresh else acc[m, :, tile] + part

    def pass_on(k):
        remote(block(k, side), block(k, side), side_send.at[k], side_recv.at[k], (e, side)).wait_recv()
        passed[k].start()

    for k in range(n // 2):
        pass_on(k)
    for j in range(n):
        remote(block(j, core), block(j, core), core_send.at[j], core_recv.at[j], (e, core)).wait_recv()
    assemble(near)
    for m in range(3):
        loads[m].wait()
        multiply(m, near, True)
        if m < 2:
            pass_on(n // 2 + m)
    for k in range(n // 2 + 2, n):
        pass_on(k)
    own_probs.wait()
    for j in range(1, n):
        remote(
            probs_ref.at[others[j]], got_probs_ref.at[others[j]], prob_send.at[j], prob_recv.at[j], (others[j], t)
        ).wait_recv()
    for s in range(n):
        prob_rows[s * cap : (s + 1) * cap, :] = got_probs_ref[s]
    for j in range(n):
        remote(block(j, far), block(j, far), pass_send.at[j], pass_recv.at[j], (e, core)).wait_recv()
    assemble(1 - near)
    for m in range(3):
        multiply(m, 1 - near, False)

    @pl.loop(0, slots // 16)
    def _(r):
        span = pl.ds(pl.multiple_of(r * 16, 16), 16)
        prob = prob_rows[span, 0:1]
        score = jnp.zeros((16, 1), jnp.float32)
        for low in range(0, hidden, 384):
            tile = slice(low, min(low + 384, hidden))
            pre_gate = acc[0, span, tile]
            pre_up = acc[1, span, tile]
            back = acc[2, span, tile]
            sigmoid = jax.nn.sigmoid(pre_gate)
            silu = pre_gate * sigmoid
            hid = (silu * pre_up).astype(jnp.bfloat16).astype(jnp.float32)
            score = score + jnp.sum(hid * back, axis=1, keepdims=True)
            scaled_ref[span, tile] = (prob * hid).astype(jnp.bfloat16)
            grad = prob * back
            gate_ref[span, tile] = (grad * pre_up * sigmoid * (1.0 + pre_gate * (1.0 - sigmoid))).astype(jnp.bfloat16)
            up_ref[span, tile] = (grad * silu).astype(jnp.bfloat16)
        score_rows[span, :] = jnp.broadcast_to(score, (16, 128))

    diagonal = lax.broadcasted_iota(jnp.int32, (cap, 128), 0) == lax.broadcasted_iota(jnp.int32, (cap, 128), 1)
    for s in range(n):
        line = jnp.sum(jnp.where(diagonal, score_rows[s * cap : (s + 1) * cap, :], 0.0), axis=0, keepdims=True)
        score_ref[s] = jnp.broadcast_to(line, score_ref.shape[1:])

    for copy in mine + small + to_core + to_side + passed:
        copy.wait_send()


def dispatch(send, probs, w_gate, w_up, w_down):
    n, double, width = send.shape
    cap = double // 2
    slots = n * cap
    hidden, full = w_gate.shape
    dma = pltpu.SemaphoreType.DMA
    small = jax.ShapeDtypeStruct((slots, hidden), jnp.bfloat16)
    return pl.pallas_call(
        functools.partial(dispatch_kernel, n),
        out_shape=(
            jax.ShapeDtypeStruct((slots, full), jnp.bfloat16),
            small,
            small,
            small,
            jax.ShapeDtypeStruct((n, 8, 128), jnp.float32),
        ),
        in_specs=[pl.BlockSpec(memory_space=VMEM)] * 2 + [pl.BlockSpec(memory_space=pl.ANY)] * 3,
        out_specs=[pl.BlockSpec(memory_space=VMEM)] * 5,
        scratch_shapes=[
            pltpu.VMEM((n, double, full), jnp.bfloat16),
            pltpu.VMEM((3, hidden, full), jnp.bfloat16),
            pltpu.VMEM((3, slots, hidden), jnp.float32),
            pltpu.VMEM((slots, full), jnp.bfloat16),
            pltpu.VMEM((slots, 128), jnp.float32),
            pltpu.VMEM((n, cap, 128), jnp.float32),
            pltpu.VMEM((slots, 128), jnp.float32),
            dma((3,)),
            dma((2,)),
        ]
        + [dma((n,))] * 10,
        compiler_params=pltpu.CompilerParams(
            collective_id=0, has_side_effects=True, vmem_limit_bytes=54 * 1024 * 1024
        ),
        cost_estimate=pl.CostEstimate(
            flops=6 * slots * full * hidden, bytes_accessed=6 * hidden * full, transcendentals=slots * hidden
        ),
    )(send, probs, w_gate, w_up, w_down)


def combine_kernel(
    n, gate_ref, up_ref, score_ref, w_gate, w_up, got_ref, got_score_ref,
    weights, keep, ship, from_core, mid, from_side, out, score_parts, score_sum,
    load_sem, core_send, core_recv, side_send, side_recv, out_send, out_recv, own_sem,
    sum_send, sum_recv, score_send, score_recv,
):
    e = lax.axis_index("expert")
    t = lax.axis_index("tensor")
    core, side, far = flip(t, 1), flip(t, 2), flip(flip(t, 1), 2)
    others = [flip_all(e, j) for j in range(n)]
    chunks, chunk, width = mid.shape
    cap = chunk // 2
    half = out.shape[2]
    quarters = (far, side, core, t)
    loads = []
    for i, quarter in enumerate(quarters):
        cols = pl.ds(pl.multiple_of(quarter * width, 128), width)
        for m, weight in enumerate((w_gate, w_up)):
            copy = pltpu.make_async_copy(weight.at[:, cols], weights.at[i, m], load_sem.at[i, m])
            copy.start()
            loads.append(copy)
    greet([(o, t) for o in others[1:]] + [(e, core), (e, side), (e, far)])
    sums = [
        remote(score_ref, score_parts.at[i], sum_send.at[i], sum_recv.at[i], (e, peer))
        for i, peer in enumerate((core, side, far))
    ]
    for copy in sums:
        copy.start()

    def product(i, dst):
        loads[2 * i].wait()
        loads[2 * i + 1].wait()

        @pl.loop(0, width // 256)
        def _(c):
            cols = pl.ds(pl.multiple_of(c * 256, 256), 256)
            dst[:, cols] = (
                jnp.dot(gate_ref[...], weights[i, 0, :, cols], preferred_element_type=jnp.float32)
                + jnp.dot(up_ref[...], weights[i, 1, :, cols], preferred_element_type=jnp.float32)
            ).astype(dst.dtype)

    def span(k):
        return pl.ds(pl.multiple_of(k * chunk, chunk), chunk)

    turns = (2, 3, 1, 0)
    pairs = [flip_all(e // 2, j) for j in range(chunks)]

    def give(i):
        copies = {}
        for j in turns:
            copies[j] = remote(
                ship.at[i, span(pairs[j])], from_core.at[i, j], core_send.at[i, j], core_recv.at[i, j], (e, core)
            )
            copies[j].start()
        return copies

    product(0, ship.at[0])
    give_far = give(0)
    product(1, keep.at[0])
    to_side = {}
    for j in turns:
        give_far[j].wait_recv()
        mid[j] = (keep[0, span(pairs[j]), :] + from_core[0, j].astype(jnp.float32)).astype(jnp.bfloat16)
        to_side[j] = remote(mid.at[j], from_side.at[j], side_send.at[j], side_recv.at[j], (e, side))
        to_side[j].start()
    product(2, ship.at[1])
    give_core = give(1)
    for copy in sums:
        copy.wait_recv()
    score_sum[...] = score_ref[...] + score_parts[0] + score_parts[1] + score_parts[2]
    own_score = pltpu.make_async_copy(score_sum.at[e], got_score_ref.at[e], own_sem.at[1])
    own_score.start()
    sent = []
    for j in range(1, n):
        copy = remote(
            score_sum.at[others[j]], got_score_ref.at[e], score_send.at[j], score_recv.at[j], (others[j], t)
        )
        copy.start()
        sent.append(copy)
    product(3, keep.at[1])
    own = pltpu.make_async_copy(out.at[0], got_ref.at[e], own_sem.at[0])
    for j in turns:
        give_core[j].wait_recv()
        to_side[j].wait_recv()
        total = (
            keep[1, span(pairs[j]), :] + from_core[1, j].astype(jnp.float32) + from_side[j].astype(jnp.float32)
        )
        low = jnp.concatenate([total[:cap, :half], total[:cap, half:]], axis=0).astype(jnp.bfloat16)
        high = jnp.concatenate([total[cap:, :half], total[cap:, half:]], axis=0).astype(jnp.bfloat16)
        odd = lax.rem(e, 2) == 1
        out[2 * j] = jnp.where(odd, high, low)
        out[2 * j + 1] = jnp.where(odd, low, high)
        for i in (2 * j, 2 * j + 1):
            if i == 0:
                own.start()
            else:
                copy = remote(out.at[i], got_ref.at[e], out_send.at[i], out_recv.at[i], (others[i], t))
                copy.start()
                sent.append(copy)
    own.wait()
    own_score.wait()
    for j in range(1, n):
        remote(out.at[j], got_ref.at[others[j]], out_send.at[j], out_recv.at[j], (others[j], t)).wait_recv()
        remote(
            score_sum.at[others[j]], got_score_ref.at[others[j]], score_send.at[j], score_recv.at[j], (others[j], t)
        ).wait_recv()
    for copy in list(give_far.values()) + list(give_core.values()) + sums + list(to_side.values()) + sent:
        copy.wait_send()


def combine(grad_gate, grad_up, scores, w_gate, w_up):
    tensor = lax.axis_size("tensor")
    slots, hidden = grad_gate.shape
    width = w_gate.shape[1] // tensor
    n = scores.shape[0]
    cap = slots // n
    chunk = 2 * cap
    dma = pltpu.SemaphoreType.DMA
    return pl.pallas_call(
        functools.partial(combine_kernel, n),
        out_shape=(
            jax.ShapeDtypeStruct((n, chunk, width // 2), jnp.bfloat16),
            jax.ShapeDtypeStruct(scores.shape, jnp.float32),
        ),
        in_specs=[pl.BlockSpec(memory_space=VMEM)] * 3 + [pl.BlockSpec(memory_space=pl.ANY)] * 2,
        out_specs=[pl.BlockSpec(memory_space=VMEM)] * 2,
        scratch_shapes=[
            pltpu.VMEM((tensor, 2, hidden, width), jnp.bfloat16),
            pltpu.VMEM((2, slots, width), jnp.float32),
            pltpu.VMEM((2, slots, width), jnp.bfloat16),
            pltpu.VMEM((2, n // 2, chunk, width), jnp.bfloat16),
            pltpu.VMEM((n // 2, chunk, width), jnp.bfloat16),
            pltpu.VMEM((n // 2, chunk, width), jnp.bfloat16),
            pltpu.VMEM((n, chunk, width // 2), jnp.bfloat16),
            pltpu.VMEM((3,) + scores.shape, jnp.float32),
            pltpu.VMEM(scores.shape, jnp.float32),
            dma((tensor, 2)),
            dma((2, n // 2)), dma((2, n // 2)),
            dma((n // 2,)), dma((n // 2,)),
            dma((n,)), dma((n,)), dma((2,)),
            dma((3,)), dma((3,)),
            dma((n,)), dma((n,)),
        ],
        compiler_params=pltpu.CompilerParams(
            collective_id=1, has_side_effects=True, vmem_limit_bytes=54 * 1024 * 1024
        ),
        cost_estimate=pl.CostEstimate(
            flops=4 * slots * hidden * width * tensor, bytes_accessed=4 * hidden * width * tensor, transcendentals=0
        ),
    )(grad_gate, grad_up, scores, w_gate, w_up)


def down_kernel(scaled_ref, dy_ref, out_ref, turned):
    @pl.when(pl.program_id(0) == 0)
    def _():
        turned[...] = scaled_ref[...].T

    out_ref[...] = jnp.dot(turned[...], dy_ref[...], preferred_element_type=jnp.float32).astype(jnp.bfloat16)


def down_product(scaled, rows_dy):
    slots, hidden = scaled.shape
    full = rows_dy.shape[1]
    tile = 512
    return pl.pallas_call(
        down_kernel,
        grid=(full // tile,),
        out_shape=jax.ShapeDtypeStruct((hidden, full), jnp.bfloat16),
        in_specs=[pl.BlockSpec((slots, hidden), lambda c: (0, 0)), pl.BlockSpec((slots, tile), lambda c: (0, c))],
        out_specs=pl.BlockSpec((hidden, tile), lambda c: (0, c)),
        scratch_shapes=[pltpu.VMEM((hidden, slots), jnp.bfloat16)],
        compiler_params=pltpu.CompilerParams(vmem_limit_bytes=24 * 1024 * 1024),
        cost_estimate=pl.CostEstimate(
            flops=2 * slots * hidden * full, bytes_accessed=2 * hidden * full, transcendentals=0
        ),
    )(scaled, rows_dy)


def per_device(tokens, grad_out, probs, routes, gate_weight, up_weight, down_weight):
    n_experts = lax.axis_size("expert")
    capacity = min(SLOTS // n_experts, TOK_DEV)
    slots = n_experts * capacity
    tok_rows, width = tokens.shape
    half = width // 2
    top_count = routes.shape[1]
    experts = lax.broadcasted_iota(jnp.int32, (tok_rows, top_count, n_experts), 2)
    named = (routes[:, :, None] == experts).astype(jnp.float32)
    earlier = (
        lax.broadcasted_iota(jnp.int32, (tok_rows, tok_rows), 0)
        > lax.broadcasted_iota(jnp.int32, (tok_rows, tok_rows), 1)
    ).astype(jnp.bfloat16)
    before = jnp.dot(earlier, named.sum(axis=1).astype(jnp.bfloat16), preferred_element_type=jnp.float32)
    position = jnp.sum(named * before[:, None, :], axis=2).astype(jnp.int32)
    pair_slot = routes * capacity + position
    across = pair_slot.T
    slot_iota = lax.broadcasted_iota(jnp.int32, (slots, tok_rows), 0)
    probs_across = probs.T.astype(jnp.float32)
    weighted = sum(
        jnp.where(across[k][None, :] == slot_iota, probs_across[k][None, :], 0.0) for k in range(top_count)
    ).astype(jnp.bfloat16)
    send_probs = jnp.dot(
        weighted, jnp.ones((tok_rows, 128), jnp.bfloat16), preferred_element_type=jnp.float32
    ).reshape(n_experts, capacity, 128)
    code = routes.T * (2 * capacity) + position.T
    code = jnp.concatenate([code, code + capacity], axis=1)
    row_iota = lax.broadcasted_iota(jnp.int32, (2 * slots, 2 * tok_rows), 0)
    placer = sum((code[k][None, :] == row_iota).astype(jnp.float32) for k in range(top_count)).astype(jnp.bfloat16)
    send = (
        jnp.dot(placer, jnp.concatenate([tokens, grad_out], axis=0), preferred_element_type=jnp.float32)
        .astype(jnp.bfloat16)
        .reshape(n_experts, 2 * capacity, width)
    )
    rows_dy, scaled, grad_gate, grad_up, score_block = dispatch(
        send, send_probs, gate_weight[0], up_weight[0], down_weight[0]
    )
    back_rows, back_scores = combine(grad_gate, grad_up, score_block, gate_weight[0], up_weight[0])
    down_grad = down_product(scaled, rows_dy)
    token_grad = lax.dot_general(
        placer, back_rows.reshape(2 * slots, half), (((0,), (0,)), ((), ())), preferred_element_type=jnp.float32
    )
    d_tokens = jnp.concatenate([token_grad[:tok_rows], token_grad[tok_rows:]], axis=1).astype(jnp.bfloat16)
    scores = back_scores[:, 0, :capacity].reshape(1, 1, slots)
    chosen = pair_slot[:, :, None] == lax.broadcasted_iota(jnp.int32, (tok_rows, top_count, slots), 2)
    d_probs = jnp.sum(jnp.where(chosen, scores, 0.0), axis=2)
    return d_tokens, d_probs, down_grad[None]


def plain_device(tokens, grad_out, probs, routes, gate_weight, up_weight, down_weight):
    n_experts = lax.axis_size("expert")
    capacity = min(SLOTS // n_experts, TOK_DEV)
    slots = n_experts * capacity
    tok_rows = routes.shape[0]
    top_count = routes.shape[1]
    flat_routes = routes.reshape(-1)
    pair_count = flat_routes.shape[0]
    experts_iota = lax.broadcasted_iota(jnp.int32, (pair_count, n_experts), 1)
    onehot = (flat_routes[:, None] == experts_iota).astype(jnp.int32)
    before = jnp.cumsum(onehot, axis=0) - onehot
    position = jnp.sum(before * onehot, axis=1)
    pair_slot = flat_routes * capacity + position
    slot_iota = lax.broadcasted_iota(jnp.int32, (slots, pair_count), 0)
    placer = (pair_slot[None, :] == slot_iota).astype(jnp.float32)
    token_placer = placer.reshape(slots, tok_rows, top_count).sum(axis=2)
    placer_half = placer.astype(jnp.bfloat16)
    token_half = token_placer.astype(jnp.bfloat16)
    send_probs = (
        jnp.dot(placer_half, probs.reshape(-1), preferred_element_type=jnp.float32)
        .astype(jnp.bfloat16)
        .reshape(n_experts, capacity)
    )
    send_x = (
        jnp.dot(token_half, tokens, preferred_element_type=jnp.float32)
        .astype(jnp.bfloat16)
        .reshape(n_experts, capacity, -1)
    )
    send_dy = (
        jnp.dot(token_half, grad_out, preferred_element_type=jnp.float32)
        .astype(jnp.bfloat16)
        .reshape(n_experts, capacity, -1)
    )
    got_x, got_dy, got_probs = (
        lax.all_to_all(send_x, "expert", split_axis=0, concat_axis=0, tiled=True),
        lax.all_to_all(send_dy, "expert", split_axis=0, concat_axis=0, tiled=True),
        lax.all_to_all(send_probs, "expert", split_axis=0, concat_axis=0, tiled=True),
    )
    rows_x, rows_dy = (
        lax.all_gather(got_x, "tensor", axis=2, tiled=True),
        lax.all_gather(got_dy, "tensor", axis=2, tiled=True),
    )
    rows_x = rows_x.reshape(slots, -1)
    rows_dy = rows_dy.reshape(slots, -1)
    prob_rows = got_probs.reshape(slots).astype(jnp.float32)
    w_gate = gate_weight[0]
    w_up = up_weight[0]
    w_down = down_weight[0]
    contract_last = (((1,), (1,)), ((), ()))
    pre_gate = lax.dot_general(rows_x, w_gate, contract_last, preferred_element_type=jnp.float32)
    pre_up = lax.dot_general(rows_x, w_up, contract_last, preferred_element_type=jnp.float32)
    sigmoid_a = jax.nn.sigmoid(pre_gate)
    silu_a = pre_gate * sigmoid_a
    hidden = (silu_a * pre_up).astype(jnp.bfloat16)
    back_hidden = lax.dot_general(
        rows_dy, w_down, contract_last, preferred_element_type=jnp.float32
    )
    score_part = jnp.sum(hidden.astype(jnp.float32) * back_hidden, axis=1)
    scaled_hidden = (prob_rows[:, None] * hidden.astype(jnp.float32)).astype(jnp.bfloat16)
    down_grad = lax.dot_general(
        scaled_hidden, rows_dy, (((0,), (0,)), ((), ())), preferred_element_type=jnp.float32
    ).astype(jnp.bfloat16)
    hidden_grad = prob_rows[:, None] * back_hidden
    grad_gate = (hidden_grad * pre_up * sigmoid_a * (1.0 + pre_gate * (1.0 - sigmoid_a))).astype(
        jnp.bfloat16
    )
    grad_up = (hidden_grad * silu_a).astype(jnp.bfloat16)
    input_grad = jnp.dot(grad_gate, w_gate, preferred_element_type=jnp.float32) + jnp.dot(
        grad_up, w_up, preferred_element_type=jnp.float32
    )
    scores = lax.psum(score_part, "tensor")
    score_block = scores.reshape(n_experts, capacity)
    grad_block = input_grad.reshape(n_experts, capacity, -1)
    placer_back = token_placer.T
    shares = lax.psum_scatter(grad_block, "tensor", scatter_dimension=2, tiled=True)
    back_rows, back_scores = (
        lax.all_to_all(shares, "expert", split_axis=0, concat_axis=0, tiled=True),
        lax.all_to_all(score_block, "expert", split_axis=0, concat_axis=0, tiled=True),
    )
    token_grad = jnp.dot(placer_back, back_rows.reshape(slots, -1), precision=lax.Precision.HIGHEST)
    d_tokens = token_grad.astype(jnp.bfloat16)
    d_probs = jnp.dot(
        placer.T, back_scores.reshape(slots), precision=lax.Precision.HIGHEST
    ).reshape(tok_rows, top_count)
    return (d_tokens, d_probs, down_grad[None])


def solution(mesh):
    regular = mesh.shape["tensor"] == 4 and mesh.shape["expert"] == 8
    return jax.shard_map(
        per_device if regular else plain_device,
        mesh=mesh,
        in_specs=(
            P("expert", "tensor"),
            P("expert", "tensor"),
            P("expert", None),
            P("expert", None),
            P("expert", "tensor", None),
            P("expert", "tensor", None),
            P("expert", "tensor", None),
        ),
        out_specs=(P("expert", "tensor"), P("expert", None), P("expert", "tensor", None)),
        check_vma=False,
    )
```

```python
import functools

import jax
import jax.numpy as jnp
from jax import lax
from jax.experimental import pallas as pl
from jax.experimental.pallas import tpu as pltpu
from jax.sharding import PartitionSpec as P

TOK_DEV = 64
SLOTS = 320
MESH_ID = pl.DeviceIdType.MESH
VMEM = pltpu.VMEM


def greet(peers):
    barrier = pltpu.get_barrier_semaphore()
    for peer in peers:
        pl.semaphore_signal(barrier, inc=1, device_id=peer, device_id_type=MESH_ID)
    pl.semaphore_wait(barrier, len(peers))


def remote(src, dst, send_sem, recv_sem, peer):
    return pltpu.make_async_remote_copy(
        src_ref=src,
        dst_ref=dst,
        send_sem=send_sem,
        recv_sem=recv_sem,
        device_id=peer,
        device_id_type=MESH_ID,
    )


def flip(index, bit):
    if bit == 0:
        return index
    return index + bit - 2 * bit * lax.rem(index // bit, 2)


def flip_all(index, number):
    for bit in (1, 2, 4, 8):
        if number & bit:
            index = flip(index, bit)
    return index


def dispatch_kernel(
    n, send_ref, probs_ref, w_gate, w_up, w_down, dy_ref, scaled_ref, gate_ref, up_ref, score_ref,
    rows, weights, acc, x_rows, score_rows, got_probs_ref, prob_rows, load_sem, own_sem, out_send, out_recv, core_send, core_recv,
    side_send, side_recv, pass_send, pass_recv, prob_send, prob_recv,
):
    e = lax.axis_index("expert")
    t = lax.axis_index("tensor")
    width = send_ref.shape[2]
    cap = send_ref.shape[1] // 2
    core, side, far = flip(t, 1), flip(t, 2), flip(flip(t, 1), 2)
    others = [flip_all(e, j) for j in range(n)]
    greet([(o, t) for o in others[1:]] + [(e, core), (e, side)])

    def columns(index):
        return pl.ds(pl.multiple_of(index * width, 128), width)

    mine = [
        remote(send_ref.at[others[j]], rows.at[e, :, columns(t)], out_send.at[j], out_recv.at[j], (others[j], t))
        for j in range(1, n)
    ]
    small = [
        remote(probs_ref.at[others[j]], got_probs_ref.at[e], prob_send.at[j], prob_recv.at[j], (others[j], t))
        for j in range(1, n)
    ]
    own = pltpu.make_async_copy(send_ref.at[e], rows.at[e, :, columns(t)], own_sem.at[0])
    own_probs = pltpu.make_async_copy(probs_ref.at[e], got_probs_ref.at[e], own_sem.at[1])
    own.start()
    own_probs.start()
    for copy in mine:
        copy.start()
    for copy in small:
        copy.start()
    loads = [
        pltpu.make_async_copy(weight, weights.at[m], load_sem.at[m]) for m, weight in enumerate((w_gate, w_up, w_down))
    ]
    for copy in loads:
        copy.start()

    def block(j, index):
        return rows.at[others[j], :, columns(index)]

    to_core = [remote(block(j, t), block(j, t), core_send.at[j], core_recv.at[j], (e, core)) for j in range(n)]
    to_side = [remote(block(j, t), block(j, t), side_send.at[j], side_recv.at[j], (e, side)) for j in range(n)]
    passed = [remote(block(j, side), block(j, side), pass_send.at[j], pass_recv.at[j], (e, core)) for j in range(n)]
    def forward(j):
        if j == 0:
            own.wait()
        else:
            remote(send_ref.at[others[j]], block(j, t), out_send.at[j], out_recv.at[j], (others[j], t)).wait_recv()
        to_side[j].start()
        to_core[j].start()

    slots = dy_ref.shape[0]
    hidden = gate_ref.shape[1]
    reach = 2 * width
    near = t // 2

    def half_columns(index):
        return pl.ds(pl.multiple_of(index * reach, 128), reach)

    group = n // 2
    group_rows = group * cap
    here = e // group

    def assemble(g, index):
        for c in range(2):
            cols = pl.ds(pl.multiple_of(index * reach + c * width, 128), width)
            for k in range(group // 2):
                source = g * group + 2 * k
                first = rows[source, :, cols].astype(jnp.float32)
                second = rows[source + 1, :, cols].astype(jnp.float32)
                span = pl.ds(pl.multiple_of(source * cap, 16), 2 * cap)
                x_rows[span, cols] = jnp.concatenate([first[:cap], second[:cap]], axis=0).astype(jnp.bfloat16)
                dy_ref[span, cols] = jnp.concatenate([first[cap:], second[cap:]], axis=0).astype(jnp.bfloat16)

    def multiply(m, g, index, fresh):
        cols = half_columns(index)
        span = pl.ds(pl.multiple_of(g * group_rows, 16), group_rows)
        for low in range(0, hidden, 512):
            tile = slice(low, min(low + 512, hidden))
            part = lax.dot_general(
                (dy_ref if m == 2 else x_rows)[span, cols],
                weights[m, tile, cols],
                (((1,), (1,)), ((), ())),
                preferred_element_type=jnp.float32,
            )
            acc[m, span, tile] = part if fresh else acc[m, span, tile] + part

    def pass_on(k):
        remote(block(k, side), block(k, side), side_send.at[k], side_recv.at[k], (e, side)).wait_recv()
        passed[k].start()

    def await_core(first, last):
        for j in range(first, last):
            remote(block(j, core), block(j, core), core_send.at[j], core_recv.at[j], (e, core)).wait_recv()

    def await_far(first, last):
        for j in range(first, last):
            remote(block(j, far), block(j, far), pass_send.at[j], pass_recv.at[j], (e, core)).wait_recv()

    def finish(g):
        @pl.loop(0, group_rows // 16)
        def _(r):
            elementwise(pl.ds(pl.multiple_of(g * group_rows + r * 16, 16), 16))

    def elementwise(span):
        prob = prob_rows[span, 0:1]
        score = jnp.zeros((16, 1), jnp.float32)
        for low in range(0, hidden, 384):
            tile = slice(low, min(low + 384, hidden))
            pre_gate = acc[0, span, tile]
            pre_up = acc[1, span, tile]
            back = acc[2, span, tile]
            sigmoid = jax.nn.sigmoid(pre_gate)
            silu = pre_gate * sigmoid
            hid = (silu * pre_up).astype(jnp.bfloat16).astype(jnp.float32)
            score = score + jnp.sum(hid * back, axis=1, keepdims=True)
            scaled_ref[span, tile] = (prob * hid).astype(jnp.bfloat16)
            grad = prob * back
            gate_ref[span, tile] = (grad * pre_up * sigmoid * (1.0 + pre_gate * (1.0 - sigmoid))).astype(jnp.bfloat16)
            up_ref[span, tile] = (grad * silu).astype(jnp.bfloat16)
        score_rows[span, :] = jnp.broadcast_to(score, (16, 128))

    for j in range(group):
        forward(j)
    await_core(0, group)
    assemble(here, near)
    for m in range(3):
        loads[m].wait()
        multiply(m, here, near, True)
        if m < 2:
            forward(group + m)
    for k in range(group):
        pass_on(k)
    for j in range(group + 2, n):
        forward(j)
    await_far(0, group)
    assemble(here, 1 - near)
    for m in range(3):
        multiply(m, here, 1 - near, False)
    pass_on(group)
    pass_on(group + 1)
    own_probs.wait()
    for j in range(1, n):
        remote(
            probs_ref.at[others[j]], got_probs_ref.at[others[j]], prob_send.at[j], prob_recv.at[j], (others[j], t)
        ).wait_recv()
    for s in range(n):
        prob_rows[s * cap : (s + 1) * cap, :] = got_probs_ref[s]
    finish(here)
    for k in range(group + 2, n):
        pass_on(k)
    await_core(group, n)
    assemble(1 - here, near)
    for m in range(3):
        multiply(m, 1 - here, near, True)
    await_far(group, n)
    assemble(1 - here, 1 - near)
    for m in range(3):
        multiply(m, 1 - here, 1 - near, False)
    finish(1 - here)

    diagonal = lax.broadcasted_iota(jnp.int32, (cap, 128), 0) == lax.broadcasted_iota(jnp.int32, (cap, 128), 1)
    for s in range(n):
        line = jnp.sum(jnp.where(diagonal, score_rows[s * cap : (s + 1) * cap, :], 0.0), axis=0, keepdims=True)
        score_ref[s] = jnp.broadcast_to(line, score_ref.shape[1:])

    for copy in mine + small + to_core + to_side + passed:
        copy.wait_send()


def dispatch(send, probs, w_gate, w_up, w_down):
    n, double, width = send.shape
    cap = double // 2
    slots = n * cap
    hidden, full = w_gate.shape
    dma = pltpu.SemaphoreType.DMA
    small = jax.ShapeDtypeStruct((slots, hidden), jnp.bfloat16)
    return pl.pallas_call(
        functools.partial(dispatch_kernel, n),
        out_shape=(
            jax.ShapeDtypeStruct((slots, full), jnp.bfloat16),
            small,
            small,
            small,
            jax.ShapeDtypeStruct((n, 8, 128), jnp.float32),
        ),
        in_specs=[pl.BlockSpec(memory_space=VMEM)] * 2 + [pl.BlockSpec(memory_space=pl.ANY)] * 3,
        out_specs=[pl.BlockSpec(memory_space=VMEM)] * 5,
        scratch_shapes=[
            pltpu.VMEM((n, double, full), jnp.bfloat16),
            pltpu.VMEM((3, hidden, full), jnp.bfloat16),
            pltpu.VMEM((3, slots, hidden), jnp.float32),
            pltpu.VMEM((slots, full), jnp.bfloat16),
            pltpu.VMEM((slots, 128), jnp.float32),
            pltpu.VMEM((n, cap, 128), jnp.float32),
            pltpu.VMEM((slots, 128), jnp.float32),
            dma((3,)),
            dma((2,)),
        ]
        + [dma((n,))] * 10,
        compiler_params=pltpu.CompilerParams(
            collective_id=0, has_side_effects=True, vmem_limit_bytes=54 * 1024 * 1024
        ),
        cost_estimate=pl.CostEstimate(
            flops=6 * slots * full * hidden, bytes_accessed=6 * hidden * full, transcendentals=slots * hidden
        ),
    )(send, probs, w_gate, w_up, w_down)


def combine_kernel(
    n, gate_ref, up_ref, score_ref, w_gate, w_up, got_ref, got_score_ref,
    weights, keep, ship, from_core, mid, from_side, out, score_parts, score_sum,
    load_sem, core_send, core_recv, side_send, side_recv, out_send, out_recv, own_sem,
    sum_send, sum_recv, score_send, score_recv,
):
    e = lax.axis_index("expert")
    t = lax.axis_index("tensor")
    core, side, far = flip(t, 1), flip(t, 2), flip(flip(t, 1), 2)
    others = [flip_all(e, j) for j in range(n)]
    chunks, chunk, width = mid.shape
    cap = chunk // 2
    half = out.shape[2]
    quarters = (far, side, core, t)
    loads = []
    for i, quarter in enumerate(quarters):
        cols = pl.ds(pl.multiple_of(quarter * width, 128), width)
        for m, weight in enumerate((w_gate, w_up)):
            copy = pltpu.make_async_copy(weight.at[:, cols], weights.at[i, m], load_sem.at[i, m])
            copy.start()
            loads.append(copy)
    greet([(o, t) for o in others[1:]] + [(e, core), (e, side), (e, far)])
    sums = [
        remote(score_ref, score_parts.at[i], sum_send.at[i], sum_recv.at[i], (e, peer))
        for i, peer in enumerate((core, side, far))
    ]
    for copy in sums:
        copy.start()

    def product(i, dst):
        loads[2 * i].wait()
        loads[2 * i + 1].wait()

        @pl.loop(0, width // 256)
        def _(c):
            cols = pl.ds(pl.multiple_of(c * 256, 256), 256)
            dst[:, cols] = (
                jnp.dot(gate_ref[...], weights[i, 0, :, cols], preferred_element_type=jnp.float32)
                + jnp.dot(up_ref[...], weights[i, 1, :, cols], preferred_element_type=jnp.float32)
            ).astype(dst.dtype)

    def span(k):
        return pl.ds(pl.multiple_of(k * chunk, chunk), chunk)

    turns = (2, 3, 1, 0)
    pairs = [flip_all(e // 2, j) for j in range(chunks)]

    def give(i):
        copies = {}
        for j in turns:
            copies[j] = remote(
                ship.at[i, span(pairs[j])], from_core.at[i, j], core_send.at[i, j], core_recv.at[i, j], (e, core)
            )
            copies[j].start()
        return copies

    product(0, ship.at[0])
    give_far = give(0)
    product(1, keep.at[0])
    to_side = {}
    for j in turns:
        give_far[j].wait_recv()
        mid[j] = (keep[0, span(pairs[j]), :] + from_core[0, j].astype(jnp.float32)).astype(jnp.bfloat16)
        to_side[j] = remote(mid.at[j], from_side.at[j], side_send.at[j], side_recv.at[j], (e, side))
        to_side[j].start()
    product(2, ship.at[1])
    give_core = give(1)
    for copy in sums:
        copy.wait_recv()
    score_sum[...] = score_ref[...] + score_parts[0] + score_parts[1] + score_parts[2]
    own_score = pltpu.make_async_copy(score_sum.at[e], got_score_ref.at[e], own_sem.at[1])
    own_score.start()
    sent = []
    for j in range(1, n):
        copy = remote(
            score_sum.at[others[j]], got_score_ref.at[e], score_send.at[j], score_recv.at[j], (others[j], t)
        )
        copy.start()
        sent.append(copy)
    product(3, keep.at[1])
    own = pltpu.make_async_copy(out.at[0], got_ref.at[e], own_sem.at[0])
    for j in turns:
        give_core[j].wait_recv()
        to_side[j].wait_recv()
        total = (
            keep[1, span(pairs[j]), :] + from_core[1, j].astype(jnp.float32) + from_side[j].astype(jnp.float32)
        )
        low = jnp.concatenate([total[:cap, :half], total[:cap, half:]], axis=0).astype(jnp.bfloat16)
        high = jnp.concatenate([total[cap:, :half], total[cap:, half:]], axis=0).astype(jnp.bfloat16)
        odd = lax.rem(e, 2) == 1
        out[2 * j] = jnp.where(odd, high, low)
        out[2 * j + 1] = jnp.where(odd, low, high)
        for i in (2 * j, 2 * j + 1):
            if i == 0:
                own.start()
            else:
                copy = remote(out.at[i], got_ref.at[e], out_send.at[i], out_recv.at[i], (others[i], t))
                copy.start()
                sent.append(copy)
    own.wait()
    own_score.wait()
    for j in range(1, n):
        remote(out.at[j], got_ref.at[others[j]], out_send.at[j], out_recv.at[j], (others[j], t)).wait_recv()
        remote(
            score_sum.at[others[j]], got_score_ref.at[others[j]], score_send.at[j], score_recv.at[j], (others[j], t)
        ).wait_recv()
    for copy in list(give_far.values()) + list(give_core.values()) + sums + list(to_side.values()) + sent:
        copy.wait_send()


def combine(grad_gate, grad_up, scores, w_gate, w_up):
    tensor = lax.axis_size("tensor")
    slots, hidden = grad_gate.shape
    width = w_gate.shape[1] // tensor
    n = scores.shape[0]
    cap = slots // n
    chunk = 2 * cap
    dma = pltpu.SemaphoreType.DMA
    return pl.pallas_call(
        functools.partial(combine_kernel, n),
        out_shape=(
            jax.ShapeDtypeStruct((n, chunk, width // 2), jnp.bfloat16),
            jax.ShapeDtypeStruct(scores.shape, jnp.float32),
        ),
        in_specs=[pl.BlockSpec(memory_space=VMEM)] * 3 + [pl.BlockSpec(memory_space=pl.ANY)] * 2,
        out_specs=[pl.BlockSpec(memory_space=VMEM)] * 2,
        scratch_shapes=[
            pltpu.VMEM((tensor, 2, hidden, width), jnp.bfloat16),
            pltpu.VMEM((2, slots, width), jnp.float32),
            pltpu.VMEM((2, slots, width), jnp.bfloat16),
            pltpu.VMEM((2, n // 2, chunk, width), jnp.bfloat16),
            pltpu.VMEM((n // 2, chunk, width), jnp.bfloat16),
            pltpu.VMEM((n // 2, chunk, width), jnp.bfloat16),
            pltpu.VMEM((n, chunk, width // 2), jnp.bfloat16),
            pltpu.VMEM((3,) + scores.shape, jnp.float32),
            pltpu.VMEM(scores.shape, jnp.float32),
            dma((tensor, 2)),
            dma((2, n // 2)), dma((2, n // 2)),
            dma((n // 2,)), dma((n // 2,)),
            dma((n,)), dma((n,)), dma((2,)),
            dma((3,)), dma((3,)),
            dma((n,)), dma((n,)),
        ],
        compiler_params=pltpu.CompilerParams(
            collective_id=1, has_side_effects=True, vmem_limit_bytes=54 * 1024 * 1024
        ),
        cost_estimate=pl.CostEstimate(
            flops=4 * slots * hidden * width * tensor, bytes_accessed=4 * hidden * width * tensor, transcendentals=0
        ),
    )(grad_gate, grad_up, scores, w_gate, w_up)


def down_kernel(scaled_ref, dy_ref, out_ref, turned):
    @pl.when(pl.program_id(0) == 0)
    def _():
        turned[...] = scaled_ref[...].T

    out_ref[...] = jnp.dot(turned[...], dy_ref[...], preferred_element_type=jnp.float32).astype(jnp.bfloat16)


def down_product(scaled, rows_dy):
    slots, hidden = scaled.shape
    full = rows_dy.shape[1]
    tile = 512
    return pl.pallas_call(
        down_kernel,
        grid=(full // tile,),
        out_shape=jax.ShapeDtypeStruct((hidden, full), jnp.bfloat16),
        in_specs=[pl.BlockSpec((slots, hidden), lambda c: (0, 0)), pl.BlockSpec((slots, tile), lambda c: (0, c))],
        out_specs=pl.BlockSpec((hidden, tile), lambda c: (0, c)),
        scratch_shapes=[pltpu.VMEM((hidden, slots), jnp.bfloat16)],
        compiler_params=pltpu.CompilerParams(vmem_limit_bytes=24 * 1024 * 1024),
        cost_estimate=pl.CostEstimate(
            flops=2 * slots * hidden * full, bytes_accessed=2 * hidden * full, transcendentals=0
        ),
    )(scaled, rows_dy)


def per_device(tokens, grad_out, probs, routes, gate_weight, up_weight, down_weight):
    n_experts = lax.axis_size("expert")
    capacity = min(SLOTS // n_experts, TOK_DEV)
    slots = n_experts * capacity
    tok_rows, width = tokens.shape
    half = width // 2
    top_count = routes.shape[1]
    experts = lax.broadcasted_iota(jnp.int32, (tok_rows, top_count, n_experts), 2)
    named = (routes[:, :, None] == experts).astype(jnp.float32)
    earlier = (
        lax.broadcasted_iota(jnp.int32, (tok_rows, tok_rows), 0)
        > lax.broadcasted_iota(jnp.int32, (tok_rows, tok_rows), 1)
    ).astype(jnp.bfloat16)
    before = jnp.dot(earlier, named.sum(axis=1).astype(jnp.bfloat16), preferred_element_type=jnp.float32)
    position = jnp.sum(named * before[:, None, :], axis=2).astype(jnp.int32)
    pair_slot = routes * capacity + position
    across = pair_slot.T
    slot_iota = lax.broadcasted_iota(jnp.int32, (slots, tok_rows), 0)
    probs_across = probs.T.astype(jnp.float32)
    weighted = sum(
        jnp.where(across[k][None, :] == slot_iota, probs_across[k][None, :], 0.0) for k in range(top_count)
    ).astype(jnp.bfloat16)
    send_probs = jnp.dot(
        weighted, jnp.ones((tok_rows, 128), jnp.bfloat16), preferred_element_type=jnp.float32
    ).reshape(n_experts, capacity, 128)
    code = routes.T * (2 * capacity) + position.T
    code = jnp.concatenate([code, code + capacity], axis=1)
    row_iota = lax.broadcasted_iota(jnp.int32, (2 * slots, 2 * tok_rows), 0)
    placer = sum((code[k][None, :] == row_iota).astype(jnp.float32) for k in range(top_count)).astype(jnp.bfloat16)
    send = (
        jnp.dot(placer, jnp.concatenate([tokens, grad_out], axis=0), preferred_element_type=jnp.float32)
        .astype(jnp.bfloat16)
        .reshape(n_experts, 2 * capacity, width)
    )
    rows_dy, scaled, grad_gate, grad_up, score_block = dispatch(
        send, send_probs, gate_weight[0], up_weight[0], down_weight[0]
    )
    back_rows, back_scores = combine(grad_gate, grad_up, score_block, gate_weight[0], up_weight[0])
    down_grad = down_product(scaled, rows_dy)
    token_grad = lax.dot_general(
        placer, back_rows.reshape(2 * slots, half), (((0,), (0,)), ((), ())), preferred_element_type=jnp.float32
    )
    d_tokens = jnp.concatenate([token_grad[:tok_rows], token_grad[tok_rows:]], axis=1).astype(jnp.bfloat16)
    scores = back_scores[:, 0, :capacity].reshape(1, 1, slots)
    chosen = pair_slot[:, :, None] == lax.broadcasted_iota(jnp.int32, (tok_rows, top_count, slots), 2)
    d_probs = jnp.sum(jnp.where(chosen, scores, 0.0), axis=2)
    return d_tokens, d_probs, down_grad[None]


def plain_device(tokens, grad_out, probs, routes, gate_weight, up_weight, down_weight):
    n_experts = lax.axis_size("expert")
    capacity = min(SLOTS // n_experts, TOK_DEV)
    slots = n_experts * capacity
    tok_rows = routes.shape[0]
    top_count = routes.shape[1]
    flat_routes = routes.reshape(-1)
    pair_count = flat_routes.shape[0]
    experts_iota = lax.broadcasted_iota(jnp.int32, (pair_count, n_experts), 1)
    onehot = (flat_routes[:, None] == experts_iota).astype(jnp.int32)
    before = jnp.cumsum(onehot, axis=0) - onehot
    position = jnp.sum(before * onehot, axis=1)
    pair_slot = flat_routes * capacity + position
    slot_iota = lax.broadcasted_iota(jnp.int32, (slots, pair_count), 0)
    placer = (pair_slot[None, :] == slot_iota).astype(jnp.float32)
    token_placer = placer.reshape(slots, tok_rows, top_count).sum(axis=2)
    placer_half = placer.astype(jnp.bfloat16)
    token_half = token_placer.astype(jnp.bfloat16)
    send_probs = (
        jnp.dot(placer_half, probs.reshape(-1), preferred_element_type=jnp.float32)
        .astype(jnp.bfloat16)
        .reshape(n_experts, capacity)
    )
    send_x = (
        jnp.dot(token_half, tokens, preferred_element_type=jnp.float32)
        .astype(jnp.bfloat16)
        .reshape(n_experts, capacity, -1)
    )
    send_dy = (
        jnp.dot(token_half, grad_out, preferred_element_type=jnp.float32)
        .astype(jnp.bfloat16)
        .reshape(n_experts, capacity, -1)
    )
    got_x, got_dy, got_probs = (
        lax.all_to_all(send_x, "expert", split_axis=0, concat_axis=0, tiled=True),
        lax.all_to_all(send_dy, "expert", split_axis=0, concat_axis=0, tiled=True),
        lax.all_to_all(send_probs, "expert", split_axis=0, concat_axis=0, tiled=True),
    )
    rows_x, rows_dy = (
        lax.all_gather(got_x, "tensor", axis=2, tiled=True),
        lax.all_gather(got_dy, "tensor", axis=2, tiled=True),
    )
    rows_x = rows_x.reshape(slots, -1)
    rows_dy = rows_dy.reshape(slots, -1)
    prob_rows = got_probs.reshape(slots).astype(jnp.float32)
    w_gate = gate_weight[0]
    w_up = up_weight[0]
    w_down = down_weight[0]
    contract_last = (((1,), (1,)), ((), ()))
    pre_gate = lax.dot_general(rows_x, w_gate, contract_last, preferred_element_type=jnp.float32)
    pre_up = lax.dot_general(rows_x, w_up, contract_last, preferred_element_type=jnp.float32)
    sigmoid_a = jax.nn.sigmoid(pre_gate)
    silu_a = pre_gate * sigmoid_a
    hidden = (silu_a * pre_up).astype(jnp.bfloat16)
    back_hidden = lax.dot_general(
        rows_dy, w_down, contract_last, preferred_element_type=jnp.float32
    )
    score_part = jnp.sum(hidden.astype(jnp.float32) * back_hidden, axis=1)
    scaled_hidden = (prob_rows[:, None] * hidden.astype(jnp.float32)).astype(jnp.bfloat16)
    down_grad = lax.dot_general(
        scaled_hidden, rows_dy, (((0,), (0,)), ((), ())), preferred_element_type=jnp.float32
    ).astype(jnp.bfloat16)
    hidden_grad = prob_rows[:, None] * back_hidden
    grad_gate = (hidden_grad * pre_up * sigmoid_a * (1.0 + pre_gate * (1.0 - sigmoid_a))).astype(
        jnp.bfloat16
    )
    grad_up = (hidden_grad * silu_a).astype(jnp.bfloat16)
    input_grad = jnp.dot(grad_gate, w_gate, preferred_element_type=jnp.float32) + jnp.dot(
        grad_up, w_up, preferred_element_type=jnp.float32
    )
    scores = lax.psum(score_part, "tensor")
    score_block = scores.reshape(n_experts, capacity)
    grad_block = input_grad.reshape(n_experts, capacity, -1)
    placer_back = token_placer.T
    shares = lax.psum_scatter(grad_block, "tensor", scatter_dimension=2, tiled=True)
    back_rows, back_scores = (
        lax.all_to_all(shares, "expert", split_axis=0, concat_axis=0, tiled=True),
        lax.all_to_all(score_block, "expert", split_axis=0, concat_axis=0, tiled=True),
    )
    token_grad = jnp.dot(placer_back, back_rows.reshape(slots, -1), precision=lax.Precision.HIGHEST)
    d_tokens = token_grad.astype(jnp.bfloat16)
    d_probs = jnp.dot(
        placer.T, back_scores.reshape(slots), precision=lax.Precision.HIGHEST
    ).reshape(tok_rows, top_count)
    return (d_tokens, d_probs, down_grad[None])


def solution(mesh):
    regular = mesh.shape["tensor"] == 4 and mesh.shape["expert"] == 8
    return jax.shard_map(
        per_device if regular else plain_device,
        mesh=mesh,
        in_specs=(
            P("expert", "tensor"),
            P("expert", "tensor"),
            P("expert", None),
            P("expert", None),
            P("expert", "tensor", None),
            P("expert", "tensor", None),
            P("expert", "tensor", None),
        ),
        out_specs=(P("expert", "tensor"), P("expert", None), P("expert", "tensor", None)),
        check_vma=False,
    )
```
